768 devices in a mesh: grp: 12 (over z), tile: 16 (over y, core), rep: 4 (over x).
Axes of the slice: x: 4, y: 8, z: 12, core: 2. Of those that a mesh axis runs over, the one named last changes fastest.
Arguments:
- amplitudes: bfloat16 [3072, 8, 4096], P(('grp', 'tile')), may hold values from -6 to 6
- tile_blocks: int32 [3072, 2], P(('grp', 'tile')), may hold values from 0 to 127, as said below
- live_rows: int32 [3072], P(('grp', 'tile')), may hold values from 4 to 8
- ladder_factors: bfloat16 [128, 2, 32, 4096], P('tile', None, 'rep'), may hold values from -0.3125 to 0.3125
- cycle_coupling: bfloat16 [64, 8, 8], replicated, may hold values from -2 to 2
- block_owner: int32 [128], replicated, may hold values from 0 to 127, as said below
Outputs:
- residual: bfloat16 [3072, 8, 4096], P(('grp', 'tile'), 'rep')
The draws below stay inside these ranges and needn't reach their ends.
Inputs may be any that keep to these rules, and one draw needn't show every extreme that they name: Column 0 is an occupied-pair block below 64, column 1 a virtual-pair block below 128. Among the tiles of one index pair of grp and tile, at most 2 have blocks whose owner position block_owner[tile_blocks[k, 1]] // 8 is the same; in every group of grp some owner has exactly 2 from every index of tile. `block_owner`: A permutation of the virtual-pair blocks.
All inputs are finite; a program needn't handle non-finite values.
Results may differ from the reference program's by a relative error of at most 0.0036.
Values may be sent and summed in bfloat16 or wider, within the bound.
No kernel may reach another device: no remote copies, remote signals or barrier semaphores. Data moves between devices by JAX's collectives and lax.ppermute only.
A program may use at most 64 MiB of HBM per device.

```python
import jax
import jax.numpy as jnp
from jax import lax

VB = 64
VV = 4096
NQ = 32
OP = 8
CAP = 2
TD = 16
VB_DEV = 8
NVB = 128
NOB = 64
TILES = 3072
N_TILE = 16


def owner_inverse(key):
    return jax.random.permutation(key, NVB)


def draw_block_owner(key, part):
    inverse = owner_inverse(key)
    return jnp.argsort(inverse).astype(jnp.int32)


def draw_tile_blocks(key, part):
    inverse = owner_inverse(key)
    key = jax.random.fold_in(key, 23)
    sources = TILES // TD
    groups = TILES // (TD * N_TILE)
    key_hot, key_src = jax.random.split(key)
    hottest = jax.random.randint(key_hot, (groups,), 0, N_TILE)
    per_source = hottest[jnp.arange(sources) // N_TILE]
    keys = jax.random.split(key_src, sources)

    def one_source(sub, heavy):
        first, second, third, fourth = jax.random.split(sub, 4)
        others = jax.random.permutation(first, (N_TILE - 1) * CAP)[:TD - CAP]
        target_rest = (heavy + 1 + others // CAP) % N_TILE
        target = jnp.concatenate([jnp.full((CAP,), heavy, jnp.int32), target_rest.astype(jnp.int32)])
        inside = jax.random.randint(second, (TD,), 0, VB_DEV)
        virtual = inverse[target * VB_DEV + inside]
        occupied = jax.random.randint(third, (TD,), 0, NOB)
        order = jax.random.permutation(fourth, TD)
        return jnp.stack([occupied[order], virtual[order]], axis=1).astype(jnp.int32)
    blocks = jax.vmap(one_source)(keys, per_source)
    return blocks.reshape(TILES, 2).astype(jnp.int32)


def touch_ends(drawn, key, smallest, largest):
    spot = [jax.random.randint(jax.random.fold_in(key, axis), (), 0, length) for axis, length in enumerate(drawn.shape)]
    longest = drawn.shape.index(max(drawn.shape))
    next_to = spot[:longest] + [(spot[longest] + 1) % drawn.shape[longest]] + spot[longest + 1:]
    return drawn.at[tuple(spot)].set(smallest).at[tuple(next_to)].set(largest)


def block_levels(own_key, shape, shards, smallest, high):
    level = 1.0
    for position, blocks in shards:
        draws = jax.random.uniform(jax.random.fold_in(jax.random.fold_in(own_key, 6), position), (blocks,), jnp.float32, smallest / len(shards), high / len(shards))
        level = level * jnp.repeat(jnp.exp(draws), shape[position] // blocks).reshape((-1,) + (1,) * (len(shape) - 1 - position))
    return level


def normal_values(stream_key, extent, scale, reach, pieces=(), dtype=jnp.bfloat16):
    drawn = scale * jax.random.normal(stream_key, extent, jnp.float32)
    if pieces:
        drawn = drawn * block_levels(stream_key, extent, pieces, -0.22, 0.18)
    return jnp.clip(drawn, -reach, reach).astype(dtype)


def setup_inputs(seed: int = 0) -> dict:
    key_list = jax.random.split(jax.random.key(seed), 7)
    return {
        "amplitudes": normal_values(key_list[0], (TILES, OP, VV), 1.0, 6.0, ((0, 192),)),
        "tile_blocks": draw_tile_blocks(jax.random.fold_in(key_list[6], 71), 0),
        "live_rows": touch_ends(jax.random.randint(key_list[2], (TILES,), OP // 2, OP + 1), jax.random.fold_in(key_list[2], 1), OP // 2, OP).astype(jnp.int32),
        "ladder_factors": normal_values(key_list[3], (NVB, 2, NQ, VV), (VB * 6) ** -0.5, 0.3125, ((0, 16), (2, 4))),
        "cycle_coupling": normal_values(key_list[4], (NOB, OP, OP), OP ** -0.5, 2.0),
        "block_owner": draw_block_owner(jax.random.fold_in(key_list[6], 71), 0),
    }


def ladder_batch(grid, factor):
    count = grid.shape[0]
    cells = grid.reshape(count, OP, VB, VB).astype(jnp.float32)
    blocks = factor.reshape(count, 2, NQ, VB, VB).astype(jnp.float32)
    middle = jnp.einsum('kqac,kpcd->kpqad', blocks[:, 0], cells).astype(jnp.bfloat16)
    middle = lax.optimization_barrier(middle).astype(jnp.float32)
    ladder = jnp.einsum('kpqad,kqbd->kpab', middle, blocks[:, 1])
    return ladder.reshape(count, OP, VV)


def reference(amplitudes, tile_blocks, live_rows, ladder_factors, cycle_coupling, block_owner):
    live = jnp.arange(OP)[None, :] < live_rows[:, None]
    masked = jnp.where(live[:, :, None], amplitudes, jnp.zeros_like(amplitudes)).astype(jnp.bfloat16)
    place = block_owner[tile_blocks[:, 1]].astype(jnp.int32)
    coupling = cycle_coupling[tile_blocks[:, 0]].astype(jnp.float32)
    batches = TILES // TD

    def one_batch(pair):
        grid, where, mix = pair
        factor = jnp.take(ladder_factors, where, axis=0)
        cycle = jnp.einsum('kpq,kqx->kpx', mix, grid.astype(jnp.float32))
        return (ladder_batch(grid, factor) + cycle).astype(jnp.bfloat16)

    result = lax.map(one_batch, (masked.reshape(batches, TD, OP, VV), place.reshape(batches, TD), coupling.reshape(batches, TD, OP, OP)))
    return result.reshape(TILES, OP, VV)
```

```python
import jax
import jax.numpy as jnp
from jax import lax
from jax.experimental import pallas as pl
from jax.experimental.pallas import tpu as pltpu
from jax.sharding import PartitionSpec as P

VB = 64
CAP = 2
GROUP = 4
LANES = 128
LABEL_ROWS = 16
UNROLL = 8
SMALL_VMEM = 16 * 1024 * 1024
LADDER_VMEM = 40 * 1024 * 1024


def low_lanes(shape):
    return lax.broadcasted_iota(jnp.int32, shape, 1) < VB


def join(first, second):
    low = low_lanes(first.shape)
    return (
        jnp.where(low, first, pltpu.roll(second, VB, 1)),
        jnp.where(low, pltpu.roll(first, VB, 1), second),
    )


def spread_rows(block, scratch):
    for t in range(block.shape[1] // LANES):
        scratch[t * 8 : (t + 1) * 8, :] = block[:, t * LANES : (t + 1) * LANES]


def factor_kernel(factor_ref, out_ref, scratch, woven):
    def one(v, carry):
        for side in range(2):
            spread_rows(factor_ref[v, side].astype(jnp.float32), scratch.at[side])
            for half in range(2):
                rows = [
                    scratch[side, pl.ds(half * GROUP + q, 32, stride=8), :] for q in range(GROUP)
                ]
                for pair in range(GROUP // 2):
                    even, odd = join(rows[2 * pair], rows[2 * pair + 1])
                    lanes = slice(pair * LANES, (pair + 1) * LANES)
                    if side == 0:
                        out_ref[half, v, 0, 0:32, lanes] = even.astype(jnp.bfloat16)
                        out_ref[half, v, 0, 32:64, lanes] = odd.astype(jnp.bfloat16)
                    else:
                        spot = half * 2 + pair
                        woven[spot, pl.ds(0, 32, stride=2), :] = even
                        woven[spot, pl.ds(1, 32, stride=2), :] = odd
                        out_ref[half, v, 1, :, lanes] = woven[spot].astype(jnp.bfloat16)
        return carry

    lax.fori_loop(0, factor_ref.shape[0], one, 0)


def arrange_factors(factors):
    owned = factors.shape[0]
    return pl.pallas_call(
        factor_kernel,
        out_shape=jax.ShapeDtypeStruct((2, owned, 2, VB, GROUP * VB), jnp.bfloat16),
        in_specs=[pl.BlockSpec(memory_space=pltpu.VMEM)],
        out_specs=pl.BlockSpec(memory_space=pltpu.VMEM),
        scratch_shapes=[
            pltpu.VMEM((2, 256, LANES), jnp.float32),
            pltpu.VMEM((4, VB, LANES), jnp.float32),
        ],
        compiler_params=pltpu.CompilerParams(vmem_limit_bytes=SMALL_VMEM),
        name="arrange_factors",
    )(factors)


def pack_kernel(
    lead_ref, blocks_ref, live_ref, owner_ref, amp_ref, out_ref, slot_ref, counts, labels, scratch, woven
):
    peers = out_ref.shape[0]
    owned = owner_ref.shape[0] // peers
    for s in range(peers):
        counts[s] = 0
        for r in range(CAP):
            labels[s, r] = 0
    out_ref[...] = jnp.zeros(out_ref.shape, out_ref.dtype)
    lead = lead_ref[0]
    for k in range(amp_ref.shape[0]):
        place = owner_ref[blocks_ref[1, k]]
        target = place // owned
        rank = counts[target]
        counts[target] = rank + 1
        labels[target, rank] = place - target * owned
        slot_ref[k] = target * CAP + rank
        spot = k % 2
        spread_rows(amp_ref[k].astype(jnp.float32), scratch.at[spot])
        live = live_ref[k]
        rows = [
            jnp.where(lead + p < live, scratch[spot, pl.ds(lead + p, 32, stride=8), :], 0.0)
            for p in range(2)
        ]
        even, odd = join(rows[0], rows[1])
        woven[spot, pl.ds(0, 32, stride=2), :] = even
        woven[spot, pl.ds(1, 32, stride=2), :] = odd
        out_ref[target, pl.ds(pl.multiple_of(rank * VB, VB), VB), :] = woven[spot].astype(jnp.bfloat16)
    row = lax.broadcasted_iota(jnp.int32, (LABEL_ROWS, LANES), 0)
    for s in range(peers):
        tag = jnp.where(row == 0, labels[s, 0], labels[s, 1])
        out_ref[s, CAP * VB :, :] = tag.astype(jnp.float32).astype(jnp.bfloat16)


def pack(lead, tile_blocks, live_rows, block_owner, amplitudes, peers):
    tiles = amplitudes.shape[0]
    smem = pl.BlockSpec(memory_space=pltpu.SMEM)
    vmem = pl.BlockSpec(memory_space=pltpu.VMEM)
    return pl.pallas_call(
        pack_kernel,
        out_shape=(
            jax.ShapeDtypeStruct((peers, CAP * VB + LABEL_ROWS, LANES), jnp.bfloat16),
            jax.ShapeDtypeStruct((tiles,), jnp.int32),
        ),
        in_specs=[smem, smem, smem, smem, vmem],
        out_specs=(vmem, smem),
        scratch_shapes=[
            pltpu.SMEM((peers,), jnp.int32),
            pltpu.SMEM((peers, CAP), jnp.int32),
            pltpu.VMEM((2, 256, LANES), jnp.float32),
            pltpu.VMEM((2, VB, LANES), jnp.float32),
        ],
        compiler_params=pltpu.CompilerParams(vmem_limit_bytes=SMALL_VMEM),
        name="pack_tiles",
    )(lead, tile_blocks, live_rows, block_owner, amplitudes)


def read_labels(buffer_ref, label_vmem, label_smem, sem):
    lane = lax.broadcasted_iota(jnp.int32, (LABEL_ROWS, LANES), 1)
    table = jnp.zeros((LABEL_ROWS, LANES), jnp.float32)
    for s in range(buffer_ref.shape[0]):
        table = jnp.where(lane == s, buffer_ref[s, CAP * VB :, :].astype(jnp.float32), table)
    label_vmem[...] = table.astype(jnp.int32)
    copy = pltpu.make_async_copy(label_vmem, label_smem, sem)
    copy.start()
    copy.wait()


def slot_terms(i, label_smem, buffer, halves):
    peer, rank = i // CAP, i % CAP
    v = label_smem[rank, peer]
    tile = buffer[peer, pl.ds(pl.multiple_of(rank * VB, VB), VB), :].astype(jnp.float32)
    turned = pltpu.roll(tile, VB, 1)
    low = low_lanes(tile.shape)
    upper = [jnp.where(low, rows, 0.0).astype(jnp.bfloat16) for rows in (tile, turned)]
    lower = [jnp.where(low, 0.0, rows).astype(jnp.bfloat16) for rows in (turned, tile)]
    pairs = jnp.concatenate([jnp.concatenate(upper, axis=1), jnp.concatenate(lower, axis=1)], axis=0)
    total = None
    for h in range(halves.shape[0]):
        left = halves[h, v, 0]
        left = jnp.concatenate([left[:, :LANES], left[:, LANES:]], axis=0)
        middle = jnp.dot(left, pairs, preferred_element_type=jnp.float32).astype(jnp.bfloat16)
        rows = [
            jnp.concatenate(
                [middle[:VB, p * LANES : (p + 1) * LANES], middle[VB:, p * LANES : (p + 1) * LANES]],
                axis=1,
            )
            for p in range(2)
        ]
        term = lax.dot_general(
            jnp.concatenate(rows, axis=0),
            halves[h, v, 1],
            (((1,), (1,)), ((), ())),
            preferred_element_type=jnp.float32,
        )
        total = term if total is None else total + term
    flat = [
        jnp.concatenate([total[p * VB : p * VB + 32], total[p * VB + 32 : (p + 1) * VB]], axis=1)
        for p in range(2)
    ]
    return jnp.concatenate(flat, axis=0)


def ladder_kernel(n, more, *refs):
    buffer_ref, half_refs = refs[0], refs[1 : 1 + n]
    earlier_ref = refs[1 + n] if more else None
    out_ref, buffer, halves, label_vmem, label_smem, sems, label_sem = refs[1 + n + more :]
    arrive = pltpu.make_async_copy(buffer_ref, buffer, sems.at[n])
    arrive.start()
    each = halves.shape[0] // n
    copies = [
        pltpu.make_async_copy(half_refs[h], halves.at[pl.ds(h * each, each)], sems.at[h]) for h in range(n)
    ]
    for copy in copies:
        copy.start()
    arrive.wait()
    read_labels(buffer, label_vmem, label_smem, label_sem)
    for copy in copies:
        copy.wait()

    def some(j, carry):
        for k in range(UNROLL):
            i = j * UNROLL + k
            terms = slot_terms(i, label_smem, buffer, halves)
            if more:
                terms = terms + earlier_ref[i]
            out_ref[i] = terms.astype(out_ref.dtype)
        return carry

    lax.fori_loop(0, out_ref.shape[0] // UNROLL, some, 0)


def ladder_terms(buffer, halves, earlier=None):
    peers = buffer.shape[0]
    slots = peers * CAP
    n, more = len(halves), int(earlier is not None)
    vmem, anywhere = pl.BlockSpec(memory_space=pltpu.VMEM), pl.BlockSpec(memory_space=pl.ANY)
    passes = slots * n * 2 * 2 * 2 * VB * VB * LANES
    return pl.pallas_call(
        lambda *refs: ladder_kernel(n, more, *refs),
        out_shape=jax.ShapeDtypeStruct((slots, VB, LANES), jnp.bfloat16 if more else jnp.float32),
        in_specs=[anywhere] * (1 + n) + [vmem] * more,
        out_specs=vmem,
        scratch_shapes=[
            pltpu.VMEM(buffer.shape, buffer.dtype),
            pltpu.VMEM((n * halves[0].shape[0],) + halves[0].shape[1:], halves[0].dtype),
            pltpu.VMEM((LABEL_ROWS, LANES), jnp.int32),
            pltpu.SMEM((LABEL_ROWS, LANES), jnp.int32),
            pltpu.SemaphoreType.DMA((n + 1,)),
            pltpu.SemaphoreType.DMA,
        ],
        compiler_params=pltpu.CompilerParams(vmem_limit_bytes=LADDER_VMEM),
        cost_estimate=pl.CostEstimate(flops=passes // 100, bytes_accessed=n << 19, transcendentals=0),
        name="ladder_terms",
    )(buffer, *halves, *([earlier] if more else []))


def finish_kernel(slot_ref, returned_ref, cycle_ref, out_ref, scratch):
    for k in range(out_ref.shape[0]):
        spot = k % 2
        block = returned_ref[slot_ref[k]].astype(jnp.float32)
        for p in range(2):
            scratch[spot, pl.ds(p, 32, stride=2), :] = block[p * 32 : (p + 1) * 32]
        for t in range(32):
            lanes = slice(t * LANES, (t + 1) * LANES)
            total = scratch[spot, 2 * t : 2 * t + 2, :] + cycle_ref[k, :, lanes]
            out_ref[k, :, lanes] = total.astype(jnp.bfloat16)


def finish(slot, returned, cycle):
    vmem = pl.BlockSpec(memory_space=pltpu.VMEM)
    return pl.pallas_call(
        finish_kernel,
        out_shape=jax.ShapeDtypeStruct(cycle.shape, jnp.bfloat16),
        in_specs=[pl.BlockSpec(memory_space=pltpu.SMEM), vmem, vmem],
        out_specs=vmem,
        scratch_shapes=[pltpu.VMEM((2, VB, LANES), jnp.float32)],
        compiler_params=pltpu.CompilerParams(vmem_limit_bytes=SMALL_VMEM),
        name="finish_tiles",
    )(slot, returned, cycle)


def cycle_terms(lead, share, amplitudes, tile_blocks, live_rows, cycle_coupling):
    tiles, rows, cells = amplitudes.shape
    chosen = (tile_blocks[:, 0:1] == jnp.arange(cycle_coupling.shape[0])[None, :]).astype(jnp.bfloat16)
    mine = lax.dynamic_slice_in_dim(cycle_coupling, lead, share, 1)
    coupling = jnp.einsum("kn,npq->kpq", chosen, mine, preferred_element_type=jnp.float32)
    live = jnp.arange(rows)[None, :] < live_rows[:, None]
    same = jnp.eye(tiles, dtype=bool)
    mixing = jnp.where(
        same[:, None, :, None] & live[:, None, None, :], coupling[:, :, None, :], 0.0
    ).astype(jnp.bfloat16)
    cycle = jnp.dot(
        mixing.reshape(tiles * share, tiles * rows),
        amplitudes.reshape(tiles * rows, cells),
        preferred_element_type=jnp.float32,
    )
    return cycle.reshape(tiles, share, cells)


def local(amplitudes, tile_blocks, live_rows, ladder_factors, cycle_coupling, block_owner):
    peers = lax.axis_size("tile")
    reps = lax.axis_size("rep")
    share = amplitudes.shape[1] // reps
    lead = lax.axis_index("rep") * share
    up = [(i, (i + 1) % reps) for i in range(reps)]
    down = [(i, (i - 1) % reps) for i in range(reps)]

    own = arrange_factors(ladder_factors)
    below = lax.ppermute(own, "rep", up)
    above = lax.ppermute(own, "rep", down)
    far_first = lax.ppermute(below[0:1], "rep", up)
    far_second = lax.ppermute(above[1:2], "rep", down)

    packed, slot = pack(
        lead.astype(jnp.int32).reshape(1), tile_blocks.T, live_rows, block_owner, amplitudes, peers
    )
    buffer = lax.all_to_all(packed, "tile", split_axis=0, concat_axis=0, tiled=True)
    cycle = cycle_terms(lead, share, amplitudes, tile_blocks, live_rows, cycle_coupling)
    earlier = ladder_terms(buffer, (own, below, above))
    terms = ladder_terms(buffer, (far_first, far_second), earlier)
    returned = lax.all_to_all(terms, "tile", split_axis=0, concat_axis=0, tiled=True)
    return finish(slot, returned, cycle)


def solution(mesh):
    placed = (
        P(("grp", "tile"), None, None),
        P(("grp", "tile"), None),
        P(("grp", "tile")),
        P("tile", None, "rep", None),
        P(),
        P(),
    )
    return jax.shard_map(
        local,
        mesh=mesh,
        in_specs=placed,
        out_specs=P(("grp", "tile"), "rep", None),
        check_vma=False,
    )
```

```python
import jax
import jax.numpy as jnp
from jax import lax
from jax.experimental import pallas as pl
from jax.experimental.pallas import tpu as pltpu
from jax.sharding import PartitionSpec as P

VB = 64
CAP = 2
GROUP = 4
LANES = 128
LABEL_ROWS = 16
FAR_UP = 9
CHUNK = 4
UNROLL = 16
PIECE = 16
OUT_SLOTS = 8
PACK_VMEM = 57 * 1024 * 1024
SMALL_VMEM = 16 * 1024 * 1024
LADDER_VMEM = 40 * 1024 * 1024


def low_lanes(shape):
    return lax.broadcasted_iota(jnp.int32, shape, 1) < VB


def join(first, second):
    low = low_lanes(first.shape)
    return (
        jnp.where(low, first, pltpu.roll(second, VB, 1)),
        jnp.where(low, pltpu.roll(first, VB, 1), second),
    )


def spread_rows(block, scratch):
    for t in range(block.shape[1] // LANES):
        scratch[t * 8 : (t + 1) * 8, :] = block[:, t * LANES : (t + 1) * LANES]


def factor_kernel(factor_ref, out_ref, scratch, woven):
    def one(v, carry):
        for side in range(2):
            spread_rows(factor_ref[v, side].astype(jnp.float32), scratch.at[side])
            for half in range(2):
                rows = [
                    scratch[side, pl.ds(half * GROUP + q, 32, stride=8), :] for q in range(GROUP)
                ]
                for pair in range(GROUP // 2):
                    even, odd = join(rows[2 * pair], rows[2 * pair + 1])
                    lanes = slice(pair * LANES, (pair + 1) * LANES)
                    if side == 0:
                        out_ref[2 * v + half, 0, 0:32, lanes] = even.astype(jnp.bfloat16)
                        out_ref[2 * v + half, 0, 32:64, lanes] = odd.astype(jnp.bfloat16)
                    else:
                        spot = half * 2 + pair
                        woven[spot, pl.ds(0, 32, stride=2), :] = even
                        woven[spot, pl.ds(1, 32, stride=2), :] = odd
                        out_ref[2 * v + half, 1, :, lanes] = woven[spot].astype(jnp.bfloat16)
        return carry

    lax.fori_loop(0, factor_ref.shape[0], one, 0)


def arrange_factors(factors):
    owned = factors.shape[0]
    return pl.pallas_call(
        factor_kernel,
        out_shape=jax.ShapeDtypeStruct((2 * owned, 2, VB, GROUP * VB), jnp.bfloat16),
        in_specs=[pl.BlockSpec(memory_space=pltpu.VMEM)],
        out_specs=pl.BlockSpec(memory_space=pltpu.VMEM),
        scratch_shapes=[
            pltpu.VMEM((2, 256, LANES), jnp.float32),
            pltpu.VMEM((4, VB, LANES), jnp.float32),
        ],
        compiler_params=pltpu.CompilerParams(vmem_limit_bytes=SMALL_VMEM),
        name="arrange_factors",
    )(factors)


def pack_kernel(
    lead_ref, blocks_hbm, live_hbm, owner_hbm, amp_hbm, out_ref, slot_ref,
    blocks_ref, live_ref, owner_ref, amp_ref, counts, labels, scratch, woven, sems,
):
    tables = [
        pltpu.make_async_copy(source, place, sems.at[k])
        for k, (source, place) in enumerate(
            ((blocks_hbm, blocks_ref), (live_hbm, live_ref), (owner_hbm, owner_ref))
        )
    ]
    tiles = amp_ref.shape[0]
    parts = [
        pltpu.make_async_copy(amp_hbm.at[pl.ds(k, CHUNK)], amp_ref.at[pl.ds(k, CHUNK)], sems.at[3 + k // CHUNK])
        for k in range(0, tiles, CHUNK)
    ]
    for copy in tables + parts:
        copy.start()
    peers = out_ref.shape[0]
    for s in range(peers):
        counts[s] = 0
        for r in range(CAP):
            labels[s, r] = 0
    out_ref[...] = jnp.zeros(out_ref.shape, out_ref.dtype)
    for copy in tables:
        copy.wait()
    owned = owner_ref.shape[0] // peers
    lead = lead_ref[0]
    for k in range(tiles):
        if k % CHUNK == 0:
            parts[k // CHUNK].wait()
        place = owner_ref[blocks_ref[1, k]]
        target = place // owned
        rank = counts[target]
        counts[target] = rank + 1
        labels[target, rank] = place - target * owned
        slot_ref[k] = target * CAP + rank
        spot = k % 2
        spread_rows(amp_ref[k].astype(jnp.float32), scratch.at[spot])
        live = live_ref[k]
        rows = [
            jnp.where(lead + p < live, scratch[spot, pl.ds(lead + p, 32, stride=8), :], 0.0)
            for p in range(2)
        ]
        even, odd = join(rows[0], rows[1])
        woven[spot, pl.ds(0, 32, stride=2), :] = even
        woven[spot, pl.ds(1, 32, stride=2), :] = odd
        out_ref[target, pl.ds(pl.multiple_of(rank * VB, VB), VB), :] = woven[spot].astype(jnp.bfloat16)
    row = lax.broadcasted_iota(jnp.int32, (LABEL_ROWS, LANES), 0)
    for s in range(peers):
        tag = jnp.where(row == 0, labels[s, 0], labels[s, 1])
        out_ref[s, CAP * VB :, :] = tag.astype(jnp.float32).astype(jnp.bfloat16)


def pack(lead, tile_blocks, live_rows, block_owner, amplitudes, peers):
    tiles = amplitudes.shape[0]
    smem = pl.BlockSpec(memory_space=pltpu.SMEM)
    vmem = pl.BlockSpec(memory_space=pltpu.VMEM)
    hbm = pl.BlockSpec(memory_space=pltpu.HBM)
    return pl.pallas_call(
        pack_kernel,
        out_shape=(
            jax.ShapeDtypeStruct((peers, CAP * VB + LABEL_ROWS, LANES), jnp.bfloat16),
            jax.ShapeDtypeStruct((tiles,), jnp.int32),
        ),
        in_specs=[smem, hbm, hbm, hbm, hbm],
        out_specs=(vmem, smem),
        scratch_shapes=[
            pltpu.SMEM(tile_blocks.shape, jnp.int32),
            pltpu.SMEM(live_rows.shape, jnp.int32),
            pltpu.SMEM(block_owner.shape, jnp.int32),
            pltpu.VMEM(amplitudes.shape, amplitudes.dtype),
            pltpu.SMEM((peers,), jnp.int32),
            pltpu.SMEM((peers, CAP), jnp.int32),
            pltpu.VMEM((2, 256, LANES), jnp.float32),
            pltpu.VMEM((2, VB, LANES), jnp.float32),
            pltpu.SemaphoreType.DMA((3 + tiles // CHUNK,)),
        ],
        compiler_params=pltpu.CompilerParams(vmem_limit_bytes=PACK_VMEM),
        name="pack_tiles",
    )(lead, tile_blocks, live_rows, block_owner, amplitudes)


def read_labels(buffer_ref, label_vmem, label_smem, sem):
    lane = lax.broadcasted_iota(jnp.int32, (LABEL_ROWS, LANES), 1)
    table = jnp.zeros((LABEL_ROWS, LANES), jnp.float32)
    for s in range(buffer_ref.shape[0]):
        table = jnp.where(lane == s, buffer_ref[s, CAP * VB :, :].astype(jnp.float32), table)
    label_vmem[...] = table.astype(jnp.int32)
    copy = pltpu.make_async_copy(label_vmem, label_smem, sem)
    copy.start()
    copy.wait()


def slot_terms(i, label_smem, buffer, held):
    peer, rank = i // CAP, i % CAP
    v = label_smem[rank, peer]
    tile = buffer[peer, pl.ds(pl.multiple_of(rank * VB, VB), VB), :].astype(jnp.float32)
    turned = pltpu.roll(tile, VB, 1)
    low = low_lanes(tile.shape)
    upper = [jnp.where(low, rows, 0.0).astype(jnp.bfloat16) for rows in (tile, turned)]
    lower = [jnp.where(low, 0.0, rows).astype(jnp.bfloat16) for rows in (turned, tile)]
    pairs = jnp.concatenate([jnp.concatenate(upper, axis=1), jnp.concatenate(lower, axis=1)], axis=0)
    total = None
    for h, half in [(h, half) for h in range(held.shape[0]) for half in range(2)]:
        left = held[h, 2 * v + half, 0]
        left = jnp.concatenate([left[:, :LANES], left[:, LANES:]], axis=0)
        middle = jnp.dot(left, pairs, preferred_element_type=jnp.float32).astype(jnp.bfloat16)
        rows = [
            jnp.concatenate(
                [middle[:VB, p * LANES : (p + 1) * LANES], middle[VB:, p * LANES : (p + 1) * LANES]],
                axis=1,
            )
            for p in range(2)
        ]
        term = lax.dot_general(
            jnp.concatenate(rows, axis=0),
            held[h, 2 * v + half, 1],
            (((1,), (1,)), ((), ())),
            preferred_element_type=jnp.float32,
        )
        total = term if total is None else total + term
    flat = [
        jnp.concatenate([total[p * VB : p * VB + 32], total[p * VB + 32 : (p + 1) * VB]], axis=1)
        for p in range(2)
    ]
    return jnp.concatenate(flat, axis=0)


def ladder_kernel(places, more, buffer, *refs):
    n = len(places)
    sources, earlier_ref = refs[:n], refs[n] if more else None
    out_ref, held, label_vmem, label_smem, sems, label_sem = refs[n + more : 6 + n + more]
    copies = []
    for source, (h, first) in zip(sources, places):
        for begin in range(0, source.shape[0], PIECE):
            count = min(PIECE, source.shape[0] - begin)
            copies.append(
                pltpu.make_async_copy(
                    source.at[pl.ds(begin, count)], held.at[h, pl.ds(first + begin, count)], sems.at[len(copies)]
                )
            )
    for copy in copies:
        copy.start()
    read_labels(buffer, label_vmem, label_smem, label_sem)
    for copy in copies:
        copy.wait()

    if not more:

        def some(j, carry):
            for k in range(UNROLL):
                i = j * UNROLL + k
                out_ref[i] = slot_terms(i, label_smem, buffer, held)
            return carry

        lax.fori_loop(0, out_ref.shape[0] // UNROLL, some, 0)
        return

    done, out_sems = refs[6 + n + more :]
    slots = done.shape[0]
    outs = [
        pltpu.make_async_copy(done.at[pl.ds(k, OUT_SLOTS)], out_ref.at[pl.ds(k, OUT_SLOTS)], out_sems.at[k // OUT_SLOTS])
        for k in range(0, slots, OUT_SLOTS)
    ]
    for i in range(slots):
        done[i] = (slot_terms(i, label_smem, buffer, held) + earlier_ref[i]).astype(done.dtype)
        if i % OUT_SLOTS == OUT_SLOTS - 1:
            outs[i // OUT_SLOTS].start()
    for copy in outs:
        copy.wait()


def ladder_terms(buffer, factors, places, earlier=None):
    slots = buffer.shape[0] * CAP
    n, more = len(factors), int(earlier is not None)
    shards = 1 + max(h for h, first in places)
    pieces = max(first + f.shape[0] for f, (h, first) in zip(factors, places))
    vmem, anywhere = pl.BlockSpec(memory_space=pltpu.VMEM), pl.BlockSpec(memory_space=pl.ANY)
    scratch = [
        pltpu.VMEM((shards, pieces) + factors[0].shape[1:], factors[0].dtype),
        pltpu.VMEM((LABEL_ROWS, LANES), jnp.int32),
        pltpu.SMEM((LABEL_ROWS, LANES), jnp.int32),
        pltpu.SemaphoreType.DMA((sum(-(-f.shape[0] // PIECE) for f in factors),)),
        pltpu.SemaphoreType.DMA,
    ]
    if more:
        scratch.append(pltpu.VMEM((slots, VB, LANES), jnp.bfloat16))
        scratch.append(pltpu.SemaphoreType.DMA((slots // OUT_SLOTS,)))
    return pl.pallas_call(
        lambda *refs: ladder_kernel(places, more, *refs),
        out_shape=jax.ShapeDtypeStruct((slots, VB, LANES), jnp.bfloat16 if more else jnp.float32),
        in_specs=[vmem] + [anywhere] * n + [vmem] * more,
        out_specs=anywhere if more else vmem,
        scratch_shapes=scratch,
        compiler_params=pltpu.CompilerParams(vmem_limit_bytes=LADDER_VMEM),
        cost_estimate=pl.CostEstimate(flops=10**7, bytes_accessed=shards << 20, transcendentals=0),
        name="ladder_terms",
    )(buffer, *factors, *([earlier] if more else []))


def finish_kernel(slot_ref, returned_ref, cycle_ref, out_ref, scratch):
    for k in range(out_ref.shape[0]):
        spot = k % 2
        block = returned_ref[slot_ref[k]].astype(jnp.float32)
        for p in range(2):
            scratch[spot, pl.ds(p, 32, stride=2), :] = block[p * 32 : (p + 1) * 32]
        for t in range(32):
            lanes = slice(t * LANES, (t + 1) * LANES)
            total = scratch[spot, 2 * t : 2 * t + 2, :] + cycle_ref[k, :, lanes]
            out_ref[k, :, lanes] = total.astype(jnp.bfloat16)


def finish(slot, returned, cycle):
    vmem = pl.BlockSpec(memory_space=pltpu.VMEM)
    return pl.pallas_call(
        finish_kernel,
        out_shape=jax.ShapeDtypeStruct(cycle.shape, jnp.bfloat16),
        in_specs=[pl.BlockSpec(memory_space=pltpu.SMEM), vmem, vmem],
        out_specs=vmem,
        scratch_shapes=[pltpu.VMEM((2, VB, LANES), jnp.float32)],
        compiler_params=pltpu.CompilerParams(vmem_limit_bytes=SMALL_VMEM),
        name="finish_tiles",
    )(slot, returned, cycle)


def cycle_terms(lead, share, amplitudes, tile_blocks, live_rows, cycle_coupling):
    tiles, rows, cells = amplitudes.shape
    chosen = (tile_blocks[:, 0:1] == jnp.arange(cycle_coupling.shape[0])[None, :]).astype(jnp.bfloat16)
    mine = lax.dynamic_slice_in_dim(cycle_coupling, lead, share, 1)
    coupling = jnp.einsum("kn,npq->kpq", chosen, mine, preferred_element_type=jnp.float32)
    live = jnp.arange(rows)[None, :] < live_rows[:, None]
    same = jnp.eye(tiles, dtype=bool)
    mixing = jnp.where(
        same[:, None, :, None] & live[:, None, None, :], coupling[:, :, None, :], 0.0
    ).astype(jnp.bfloat16)
    cycle = jnp.dot(
        mixing.reshape(tiles * share, tiles * rows),
        amplitudes.reshape(tiles * rows, cells),
        preferred_element_type=jnp.float32,
    )
    return cycle.reshape(tiles, share, cells)


def local(amplitudes, tile_blocks, live_rows, ladder_factors, cycle_coupling, block_owner):
    peers = lax.axis_size("tile")
    reps = lax.axis_size("rep")
    share = amplitudes.shape[1] // reps
    lead = lax.axis_index("rep") * share
    up = [(i, (i + 1) % reps) for i in range(reps)]
    down = [(i, (i - 1) % reps) for i in range(reps)]

    own = arrange_factors(ladder_factors)
    below = lax.ppermute(own, "rep", up)
    above = lax.ppermute(own, "rep", down)
    far_first = lax.ppermute(below[:FAR_UP], "rep", up)
    far_second = lax.ppermute(above[FAR_UP:], "rep", down)

    packed, slot = pack(
        lead.astype(jnp.int32).reshape(1), tile_blocks.T, live_rows, block_owner, amplitudes, peers
    )
    buffer = lax.all_to_all(packed, "tile", split_axis=0, concat_axis=0, tiled=True)
    cycle = cycle_terms(lead, share, amplitudes, tile_blocks, live_rows, cycle_coupling)
    earlier = ladder_terms(buffer, (own, below, above), ((0, 0), (1, 0), (2, 0)))
    terms = ladder_terms(buffer, (far_first, far_second), ((0, 0), (0, FAR_UP)), earlier)
    returned = lax.all_to_all(terms, "tile", split_axis=0, concat_axis=0, tiled=True)
    return finish(slot, returned, cycle)


def solution(mesh):
    placed = (
        P(("grp", "tile"), None, None),
        P(("grp", "tile"), None),
        P(("grp", "tile")),
        P("tile", None, "rep", None),
        P(),
        P(),
    )
    return jax.shard_map(
        local,
        mesh=mesh,
        in_specs=placed,
        out_specs=P(("grp", "tile"), "rep", None),
        check_vma=False,
    )
```

```python
import jax
import jax.numpy as jnp
from jax import lax
from jax.experimental import pallas as pl
from jax.experimental.pallas import tpu as pltpu
from jax.sharding import PartitionSpec as P

VB = 64
CAP = 2
GROUP = 4
LANES = 128
LABEL_ROWS = 16
RELAY_FLOPS = 10**9
CHUNK = 8
UNROLL = 32
OUT_SLOTS = 8
PACK_VMEM = 57 * 1024 * 1024
SMALL_VMEM = 16 * 1024 * 1024
LADDER_VMEM = 40 * 1024 * 1024


def low_lanes(shape):
    return lax.broadcasted_iota(jnp.int32, shape, 1) < VB


def join(first, second):
    low = low_lanes(first.shape)
    return (
        jnp.where(low, first, pltpu.roll(second, VB, 1)),
        jnp.where(low, pltpu.roll(first, VB, 1), second),
    )


def spread_rows(block, scratch):
    for t in range(block.shape[1] // LANES):
        scratch[t * 8 : (t + 1) * 8, :] = block[:, t * LANES : (t + 1) * LANES]


def factor_kernel(parity_ref, factor_ref, alpha_ref, beta_ref, scratch, woven):
    parity = parity_ref[0]

    def one(v, carry):
        for side in range(2):
            spread_rows(factor_ref[v, side].astype(jnp.float32), scratch.at[side])
            for half, out_ref in enumerate((alpha_ref, beta_ref)):
                begin = ((parity + half) % 2) * GROUP
                rows = [scratch[side, pl.ds(begin + q, 32, stride=8), :] for q in range(GROUP)]
                for pair in range(GROUP // 2):
                    even, odd = join(rows[2 * pair], rows[2 * pair + 1])
                    lanes = slice(pair * LANES, (pair + 1) * LANES)
                    if side == 0:
                        turned = jnp.concatenate([even, odd], axis=0).astype(jnp.bfloat16)
                    else:
                        spot = half * 2 + pair
                        woven[spot, pl.ds(0, 32, stride=2), :] = even
                        woven[spot, pl.ds(1, 32, stride=2), :] = odd
                        turned = woven[spot].astype(jnp.bfloat16)
                    out_ref[v, side, :, lanes] = turned
        return carry

    lax.fori_loop(0, factor_ref.shape[0], one, 0, unroll=4)


def arrange_factors(parity, factors):
    owned = factors.shape[0]
    return pl.pallas_call(
        factor_kernel,
        out_shape=(jax.ShapeDtypeStruct((owned, 2, VB, GROUP * VB), jnp.bfloat16),) * 2,
        in_specs=[pl.BlockSpec(memory_space=pltpu.SMEM), pl.BlockSpec(memory_space=pltpu.VMEM)],
        out_specs=(pl.BlockSpec(memory_space=pltpu.VMEM),) * 2,
        scratch_shapes=[
            pltpu.VMEM((2, 256, LANES), jnp.float32),
            pltpu.VMEM((4, VB, LANES), jnp.float32),
        ],
        compiler_params=pltpu.CompilerParams(vmem_limit_bytes=SMALL_VMEM),
        name="arrange_factors",
    )(parity, factors)


def arrived(*pieces):
    def kernel(*refs):
        refs[-1][...] = jnp.zeros(refs[-1].shape, refs[-1].dtype)

    return pl.pallas_call(
        kernel,
        out_shape=jax.ShapeDtypeStruct((8, LANES), jnp.float32),
        in_specs=[pl.BlockSpec(memory_space=pl.ANY)] * len(pieces),
        out_specs=pl.BlockSpec(memory_space=pltpu.VMEM),
        cost_estimate=pl.CostEstimate(flops=RELAY_FLOPS, bytes_accessed=8, transcendentals=0),
        name="arrived",
    )(*pieces)


def pack_kernel(
    lead_ref, blocks_hbm, live_hbm, owner_hbm, amp_hbm, out_ref, slot_ref,
    blocks_ref, live_ref, owner_ref, amp_ref, counts, labels, scratch, woven, sems,
):
    tables = [
        pltpu.make_async_copy(source, place, sems.at[k])
        for k, (source, place) in enumerate(
            ((blocks_hbm, blocks_ref), (live_hbm, live_ref), (owner_hbm, owner_ref))
        )
    ]
    tiles = amp_ref.shape[0]
    parts = [
        pltpu.make_async_copy(amp_hbm.at[pl.ds(k, CHUNK)], amp_ref.at[pl.ds(k, CHUNK)], sems.at[3 + k // CHUNK])
        for k in range(0, tiles, CHUNK)
    ]
    for copy in tables + parts:
        copy.start()
    peers = out_ref.shape[0]
    for s in range(peers):
        counts[s] = 0
        for r in range(CAP):
            labels[s, r] = 0
    out_ref[...] = jnp.zeros(out_ref.shape, out_ref.dtype)
    for copy in tables:
        copy.wait()
    owned = owner_ref.shape[0] // peers
    lead = lead_ref[0]
    for k in range(tiles):
        if k % CHUNK == 0:
            parts[k // CHUNK].wait()
        place = owner_ref[blocks_ref[1, k]]
        target = place // owned
        rank = counts[target]
        counts[target] = rank + 1
        labels[target, rank] = place - target * owned
        slot_ref[k] = target * CAP + rank
        spot = k % 2
        spread_rows(amp_ref[k].astype(jnp.float32), scratch.at[spot])
        live = live_ref[k]
        rows = [
            jnp.where(lead + p < live, scratch[spot, pl.ds(lead + p, 32, stride=8), :], 0.0)
            for p in range(2)
        ]
        even, odd = join(rows[0], rows[1])
        woven[spot, pl.ds(0, 32, stride=2), :] = even
        woven[spot, pl.ds(1, 32, stride=2), :] = odd
        out_ref[target, pl.ds(pl.multiple_of(rank * VB, VB), VB), :] = woven[spot].astype(jnp.bfloat16)
    row = lax.broadcasted_iota(jnp.int32, (LABEL_ROWS, LANES), 0)
    for s in range(peers):
        tag = jnp.where(row == 0, labels[s, 0], labels[s, 1])
        out_ref[s, CAP * VB :, :] = tag.astype(jnp.float32).astype(jnp.bfloat16)


def pack(lead, tile_blocks, live_rows, block_owner, amplitudes, peers):
    tiles = amplitudes.shape[0]
    smem = pl.BlockSpec(memory_space=pltpu.SMEM)
    vmem = pl.BlockSpec(memory_space=pltpu.VMEM)
    hbm = pl.BlockSpec(memory_space=pltpu.HBM)
    return pl.pallas_call(
        pack_kernel,
        out_shape=(
            jax.ShapeDtypeStruct((peers, CAP * VB + LABEL_ROWS, LANES), jnp.bfloat16),
            jax.ShapeDtypeStruct((tiles,), jnp.int32),
        ),
        in_specs=[smem, hbm, hbm, hbm, hbm],
        out_specs=(vmem, smem),
        scratch_shapes=[
            pltpu.SMEM(tile_blocks.shape, jnp.int32),
            pltpu.SMEM(live_rows.shape, jnp.int32),
            pltpu.SMEM(block_owner.shape, jnp.int32),
            pltpu.VMEM(amplitudes.shape, amplitudes.dtype),
            pltpu.SMEM((peers,), jnp.int32),
            pltpu.SMEM((peers, CAP), jnp.int32),
            pltpu.VMEM((2, 256, LANES), jnp.float32),
            pltpu.VMEM((2, VB, LANES), jnp.float32),
            pltpu.SemaphoreType.DMA((3 + tiles // CHUNK,)),
        ],
        compiler_params=pltpu.CompilerParams(vmem_limit_bytes=PACK_VMEM),
        name="pack_tiles",
    )(lead, tile_blocks, live_rows, block_owner, amplitudes)


def read_labels(buffer_ref, label_vmem, label_smem, sem):
    lane = lax.broadcasted_iota(jnp.int32, (LABEL_ROWS, LANES), 1)
    table = jnp.zeros((LABEL_ROWS, LANES), jnp.float32)
    for s in range(buffer_ref.shape[0]):
        table = jnp.where(lane == s, buffer_ref[s, CAP * VB :, :].astype(jnp.float32), table)
    label_vmem[...] = table.astype(jnp.int32)
    copy = pltpu.make_async_copy(label_vmem, label_smem, sem)
    copy.start()
    copy.wait()


def slot_terms(i, label_smem, buffer, held):
    peer, rank = i // CAP, i % CAP
    v = label_smem[rank, peer]
    tile = buffer[peer, pl.ds(pl.multiple_of(rank * VB, VB), VB), :].astype(jnp.float32)
    turned = pltpu.roll(tile, VB, 1)
    low = low_lanes(tile.shape)
    upper = [jnp.where(low, rows, 0.0).astype(jnp.bfloat16) for rows in (tile, turned)]
    lower = [jnp.where(low, 0.0, rows).astype(jnp.bfloat16) for rows in (turned, tile)]
    pairs = jnp.concatenate([jnp.concatenate(upper, axis=1), jnp.concatenate(lower, axis=1)], axis=0)
    total = None
    for h in range(held.shape[0]):
        left = held[h, v, 0]
        left = jnp.concatenate([left[:, :LANES], left[:, LANES:]], axis=0)
        middle = jnp.dot(left, pairs, preferred_element_type=jnp.float32).astype(jnp.bfloat16)
        rows = [
            jnp.concatenate(
                [middle[:VB, p * LANES : (p + 1) * LANES], middle[VB:, p * LANES : (p + 1) * LANES]],
                axis=1,
            )
            for p in range(2)
        ]
        term = lax.dot_general(
            jnp.concatenate(rows, axis=0),
            held[h, v, 1],
            (((1,), (1,)), ((), ())),
            preferred_element_type=jnp.float32,
        )
        total = term if total is None else total + term
    flat = [
        jnp.concatenate([total[p * VB : p * VB + 32], total[p * VB + 32 : (p + 1) * VB]], axis=1)
        for p in range(2)
    ]
    return jnp.concatenate(flat, axis=0)


def ladder_kernel(places, more, buffer, *refs):
    n = len(places)
    sources, earlier_ref = refs[:n], refs[n]
    out_ref, held, label_vmem, label_smem, sems, label_sem = refs[n + 1 : 7 + n]
    copies = [
        pltpu.make_async_copy(
            source, held.at[pl.ds(h, source.shape[0])] if len(source.shape) > 4 else held.at[h], sems.at[k]
        )
        for k, (source, h) in enumerate(zip(sources, places))
    ]
    for copy in copies:
        copy.start()
    read_labels(buffer, label_vmem, label_smem, label_sem)
    for copy in copies:
        copy.wait()

    if not more:

        def some(j, carry):
            for k in range(UNROLL):
                i = j * UNROLL + k
                out_ref[i] = slot_terms(i, label_smem, buffer, held)
            return carry

        lax.fori_loop(0, out_ref.shape[0] // UNROLL, some, 0)
        return

    done, out_sems = refs[7 + n :]
    slots = done.shape[0]
    outs = [
        pltpu.make_async_copy(done.at[pl.ds(k, OUT_SLOTS)], out_ref.at[pl.ds(k, OUT_SLOTS)], out_sems.at[k // OUT_SLOTS])
        for k in range(0, slots, OUT_SLOTS)
    ]
    for i in range(slots):
        done[i] = (slot_terms(i, label_smem, buffer, held) + earlier_ref[i]).astype(done.dtype)
        if i % OUT_SLOTS == OUT_SLOTS - 1:
            outs[i // OUT_SLOTS].start()
    for copy in outs:
        copy.wait()


def ladder_terms(buffer, factors, earlier=None, mark=None):
    slots = buffer.shape[0] * CAP
    n, more = len(factors), int(earlier is not None)
    last = earlier if more else mark
    counts = [f.shape[0] if len(f.shape) > 4 else 1 for f in factors]
    places = [sum(counts[:k]) for k in range(n)]
    vmem, anywhere = pl.BlockSpec(memory_space=pltpu.VMEM), pl.BlockSpec(memory_space=pl.ANY)
    scratch = [
        pltpu.VMEM((sum(counts),) + factors[0].shape[-4:], factors[0].dtype),
        pltpu.VMEM((LABEL_ROWS, LANES), jnp.int32),
        pltpu.SMEM((LABEL_ROWS, LANES), jnp.int32),
        pltpu.SemaphoreType.DMA((n,)),
        pltpu.SemaphoreType.DMA,
    ]
    if more:
        scratch.append(pltpu.VMEM((slots, VB, LANES), jnp.bfloat16))
        scratch.append(pltpu.SemaphoreType.DMA((slots // OUT_SLOTS,)))
    return pl.pallas_call(
        lambda *refs: ladder_kernel(places, more, *refs),
        out_shape=jax.ShapeDtypeStruct((slots, VB, LANES), jnp.bfloat16 if more else jnp.float32),
        in_specs=[vmem] + [anywhere] * n + [vmem if more else anywhere],
        out_specs=anywhere if more else vmem,
        scratch_shapes=scratch,
        compiler_params=pltpu.CompilerParams(vmem_limit_bytes=LADDER_VMEM),
        cost_estimate=pl.CostEstimate(flops=10**7, bytes_accessed=sum(counts) << 19, transcendentals=0),
        name="ladder_terms",
    )(buffer, *factors, last)


def finish_kernel(slot_ref, returned_ref, cycle_ref, out_ref, scratch):
    for g in range(out_ref.shape[0] // 4):
        spot = g % 2
        for j in range(4):
            block = returned_ref[slot_ref[4 * g + j]].astype(jnp.float32)
            for p in range(2):
                scratch[spot, pl.ds(2 * j + p, 32, stride=8), :] = block[p * 32 : (p + 1) * 32]
        for t in range(32):
            lanes = slice(t * LANES, (t + 1) * LANES)
            total = scratch[spot, 8 * t : 8 * t + 8, :] + cycle_ref[8 * g : 8 * g + 8, lanes]
            for j in range(4):
                out_ref[4 * g + j, :, lanes] = total[2 * j : 2 * j + 2].astype(jnp.bfloat16)


def finish(slot, returned, cycle):
    vmem = pl.BlockSpec(memory_space=pltpu.VMEM)
    return pl.pallas_call(
        finish_kernel,
        out_shape=jax.ShapeDtypeStruct((cycle.shape[0] // 2, 2, cycle.shape[1]), jnp.bfloat16),
        in_specs=[pl.BlockSpec(memory_space=pltpu.SMEM), vmem, vmem],
        out_specs=vmem,
        scratch_shapes=[pltpu.VMEM((2, 256, LANES), jnp.float32)],
        compiler_params=pltpu.CompilerParams(vmem_limit_bytes=SMALL_VMEM),
        name="finish_tiles",
    )(slot, returned, cycle)


def cycle_terms(lead, share, amplitudes, tile_blocks, live_rows, cycle_coupling):
    tiles, rows, cells = amplitudes.shape
    chosen = (tile_blocks[:, 0:1] == jnp.arange(cycle_coupling.shape[0])[None, :]).astype(jnp.bfloat16)
    mine = lax.dynamic_slice_in_dim(cycle_coupling, lead, share, 1)
    coupling = jnp.einsum("kn,npq->kpq", chosen, mine, preferred_element_type=jnp.float32)
    live = jnp.arange(rows)[None, :] < live_rows[:, None]
    same = jnp.eye(tiles, dtype=bool)
    mixing = jnp.where(
        same[:, None, :, None] & live[:, None, None, :], coupling[:, :, None, :], 0.0
    ).astype(jnp.bfloat16)
    return jnp.dot(
        mixing.reshape(tiles * share, tiles * rows),
        amplitudes.reshape(tiles * rows, cells),
        preferred_element_type=jnp.float32,
    )


def local(amplitudes, tile_blocks, live_rows, ladder_factors, cycle_coupling, block_owner):
    peers = lax.axis_size("tile")
    reps = lax.axis_size("rep")
    share = amplitudes.shape[1] // reps
    lead = lax.axis_index("rep") * share
    up = [(i, (i + 1) % reps) for i in range(reps)]
    down = [(i, (i - 1) % reps) for i in range(reps)]

    groups = lax.axis_size("grp")
    next_group = [(i, (i + 1) % groups) for i in range(groups)]
    last_group = [(i, (i - 1) % groups) for i in range(groups)]
    parity = (lax.axis_index("grp") % 2).astype(jnp.int32).reshape(1)

    alpha, beta = arrange_factors(parity, ladder_factors)
    below_beta = lax.ppermute(beta, "rep", up)
    above_alpha = lax.ppermute(alpha, "rep", down)
    far_beta = lax.ppermute(below_beta, "rep", up)
    far_alpha = lax.ppermute(above_alpha, "rep", down)
    below_alpha = lax.ppermute(below_beta, "grp", next_group)
    above_beta = lax.ppermute(above_alpha, "grp", last_group)

    packed, slot = pack(
        lead.astype(jnp.int32).reshape(1), tile_blocks.T, live_rows, block_owner, amplitudes, peers
    )
    buffer = lax.all_to_all(packed, "tile", split_axis=0, concat_axis=0, tiled=True)
    earlier = ladder_terms(buffer, (alpha, beta, below_beta, above_alpha, far_beta, far_alpha), mark=arrived(far_beta, far_alpha))
    terms = ladder_terms(buffer, (below_alpha, above_beta), earlier)
    tile_blocks, live_rows, terms = lax.optimization_barrier((tile_blocks, live_rows, terms))
    cycle = cycle_terms(lead, share, amplitudes, tile_blocks, live_rows, cycle_coupling)
    returned = lax.all_to_all(terms, "tile", split_axis=0, concat_axis=0, tiled=True)
    return finish(slot, returned, cycle)


def solution(mesh):
    placed = (
        P(("grp", "tile"), None, None),
        P(("grp", "tile"), None),
        P(("grp", "tile")),
        P("tile", None, "rep", None),
        P(),
        P(),
    )
    return jax.shard_map(
        local,
        mesh=mesh,
        in_specs=placed,
        out_specs=P(("grp", "tile"), "rep", None),
        check_vma=False,
    )
```

```python
import jax
import jax.numpy as jnp
from jax import lax
from jax.experimental import pallas as pl
from jax.experimental.pallas import tpu as pltpu
from jax.sharding import PartitionSpec as P

VB = 64
CAP = 2
GROUP = 4
LANES = 128
LABEL_ROWS = 16
RELAY_FLOPS = 10**9
CHUNK = 8
UNROLL = 32
OUT_SLOTS = 8
PACK_VMEM = 57 * 1024 * 1024
SMALL_VMEM = 16 * 1024 * 1024
LADDER_VMEM = 40 * 1024 * 1024


def low_lanes(shape):
    return lax.broadcasted_iota(jnp.int32, shape, 1) < VB


def join(first, second):
    low = low_lanes(first.shape)
    return (
        jnp.where(low, first, pltpu.roll(second, VB, 1)),
        jnp.where(low, pltpu.roll(first, VB, 1), second),
    )


def spread_rows(block, scratch):
    for t in range(block.shape[1] // LANES):
        scratch[t * 8 : (t + 1) * 8, :] = block[:, t * LANES : (t + 1) * LANES]


def factor_kernel(factor_ref, both_ref, second_ref, scratch, woven):
    def one(v, carry):
        for side in range(2):
            spread_rows(factor_ref[v, side].astype(jnp.float32), scratch.at[side])
            for half in range(2):
                rows = [
                    scratch[side, pl.ds(half * GROUP + q, 32, stride=8), :] for q in range(GROUP)
                ]
                for pair in range(GROUP // 2):
                    even, odd = join(rows[2 * pair], rows[2 * pair + 1])
                    lanes = slice(pair * LANES, (pair + 1) * LANES)
                    if side == 0:
                        turned = jnp.concatenate([even, odd], axis=0).astype(jnp.bfloat16)
                    else:
                        spot = half * 2 + pair
                        woven[spot, pl.ds(0, 32, stride=2), :] = even
                        woven[spot, pl.ds(1, 32, stride=2), :] = odd
                        turned = woven[spot].astype(jnp.bfloat16)
                    both_ref[half, v, side, :, lanes] = turned
                    if half == 1:
                        second_ref[v, side, :, lanes] = turned
        return carry

    lax.fori_loop(0, factor_ref.shape[0], one, 0, unroll=4)


def arrange_factors(factors):
    owned = factors.shape[0]
    return pl.pallas_call(
        factor_kernel,
        out_shape=tuple(
            jax.ShapeDtypeStruct(lead + (owned, 2, VB, GROUP * VB), jnp.bfloat16) for lead in ((2,), ())
        ),
        in_specs=[pl.BlockSpec(memory_space=pltpu.VMEM)],
        out_specs=(pl.BlockSpec(memory_space=pltpu.VMEM),) * 2,
        scratch_shapes=[
            pltpu.VMEM((2, 256, LANES), jnp.float32),
            pltpu.VMEM((4, VB, LANES), jnp.float32),
        ],
        compiler_params=pltpu.CompilerParams(vmem_limit_bytes=SMALL_VMEM),
        name="arrange_factors",
    )(factors)


def relay_kernel(piece_ref, out_ref, sem):
    copy = pltpu.make_async_copy(piece_ref, out_ref, sem)
    copy.start()
    copy.wait()


def relay(piece):
    vmem = pl.BlockSpec(memory_space=pltpu.VMEM)
    return pl.pallas_call(
        relay_kernel,
        out_shape=jax.ShapeDtypeStruct(piece.shape, piece.dtype),
        in_specs=[vmem],
        out_specs=vmem,
        scratch_shapes=[pltpu.SemaphoreType.DMA],
        cost_estimate=pl.CostEstimate(flops=RELAY_FLOPS, bytes_accessed=8, transcendentals=0),
        name="relay",
    )(piece)


def pack_kernel(
    lead_ref, blocks_hbm, live_hbm, owner_hbm, amp_hbm, out_ref, slot_ref,
    blocks_ref, live_ref, owner_ref, amp_ref, counts, labels, scratch, woven, sems,
):
    tables = [
        pltpu.make_async_copy(source, place, sems.at[k])
        for k, (source, place) in enumerate(
            ((blocks_hbm, blocks_ref), (live_hbm, live_ref), (owner_hbm, owner_ref))
        )
    ]
    tiles = amp_ref.shape[0]
    parts = [
        pltpu.make_async_copy(amp_hbm.at[pl.ds(k, CHUNK)], amp_ref.at[pl.ds(k, CHUNK)], sems.at[3 + k // CHUNK])
        for k in range(0, tiles, CHUNK)
    ]
    for copy in tables + parts:
        copy.start()
    peers = out_ref.shape[0]
    for s in range(peers):
        counts[s] = 0
        for r in range(CAP):
            labels[s, r] = 0
    out_ref[...] = jnp.zeros(out_ref.shape, out_ref.dtype)
    for copy in tables:
        copy.wait()
    owned = owner_ref.shape[0] // peers
    lead = lead_ref[0]
    for k in range(tiles):
        if k % CHUNK == 0:
            parts[k // CHUNK].wait()
        place = owner_ref[blocks_ref[1, k]]
        target = place // owned
        rank = counts[target]
        counts[target] = rank + 1
        labels[target, rank] = place - target * owned
        slot_ref[k] = target * CAP + rank
        spot = k % 2
        spread_rows(amp_ref[k].astype(jnp.float32), scratch.at[spot])
        live = live_ref[k]
        rows = [
            jnp.where(lead + p < live, scratch[spot, pl.ds(lead + p, 32, stride=8), :], 0.0)
            for p in range(2)
        ]
        even, odd = join(rows[0], rows[1])
        woven[spot, pl.ds(0, 32, stride=2), :] = even
        woven[spot, pl.ds(1, 32, stride=2), :] = odd
        out_ref[target, pl.ds(pl.multiple_of(rank * VB, VB), VB), :] = woven[spot].astype(jnp.bfloat16)
    row = lax.broadcasted_iota(jnp.int32, (LABEL_ROWS, LANES), 0)
    for s in range(peers):
        tag = jnp.where(row == 0, labels[s, 0], labels[s, 1])
        out_ref[s, CAP * VB :, :] = tag.astype(jnp.float32).astype(jnp.bfloat16)


def pack(lead, tile_blocks, live_rows, block_owner, amplitudes, peers):
    tiles = amplitudes.shape[0]
    smem = pl.BlockSpec(memory_space=pltpu.SMEM)
    vmem = pl.BlockSpec(memory_space=pltpu.VMEM)
    hbm = pl.BlockSpec(memory_space=pltpu.HBM)
    return pl.pallas_call(
        pack_kernel,
        out_shape=(
            jax.ShapeDtypeStruct((peers, CAP * VB + LABEL_ROWS, LANES), jnp.bfloat16),
            jax.ShapeDtypeStruct((tiles,), jnp.int32),
        ),
        in_specs=[smem, hbm, hbm, hbm, hbm],
        out_specs=(vmem, smem),
        scratch_shapes=[
            pltpu.SMEM(tile_blocks.shape, jnp.int32),
            pltpu.SMEM(live_rows.shape, jnp.int32),
            pltpu.SMEM(block_owner.shape, jnp.int32),
            pltpu.VMEM(amplitudes.shape, amplitudes.dtype),
            pltpu.SMEM((peers,), jnp.int32),
            pltpu.SMEM((peers, CAP), jnp.int32),
            pltpu.VMEM((2, 256, LANES), jnp.float32),
            pltpu.VMEM((2, VB, LANES), jnp.float32),
            pltpu.SemaphoreType.DMA((3 + tiles // CHUNK,)),
        ],
        compiler_params=pltpu.CompilerParams(vmem_limit_bytes=PACK_VMEM),
        name="pack_tiles",
    )(lead, tile_blocks, live_rows, block_owner, amplitudes)


def read_labels(buffer_ref, label_vmem, label_smem, sem):
    lane = lax.broadcasted_iota(jnp.int32, (LABEL_ROWS, LANES), 1)
    table = jnp.zeros((LABEL_ROWS, LANES), jnp.float32)
    for s in range(buffer_ref.shape[0]):
        table = jnp.where(lane == s, buffer_ref[s, CAP * VB :, :].astype(jnp.float32), table)
    label_vmem[...] = table.astype(jnp.int32)
    copy = pltpu.make_async_copy(label_vmem, label_smem, sem)
    copy.start()
    copy.wait()


def slot_terms(i, label_smem, buffer, held):
    peer, rank = i // CAP, i % CAP
    v = label_smem[rank, peer]
    tile = buffer[peer, pl.ds(pl.multiple_of(rank * VB, VB), VB), :].astype(jnp.float32)
    turned = pltpu.roll(tile, VB, 1)
    low = low_lanes(tile.shape)
    upper = [jnp.where(low, rows, 0.0).astype(jnp.bfloat16) for rows in (tile, turned)]
    lower = [jnp.where(low, 0.0, rows).astype(jnp.bfloat16) for rows in (turned, tile)]
    pairs = jnp.concatenate([jnp.concatenate(upper, axis=1), jnp.concatenate(lower, axis=1)], axis=0)
    total = None
    for h in range(held.shape[0]):
        left = held[h, v, 0]
        left = jnp.concatenate([left[:, :LANES], left[:, LANES:]], axis=0)
        middle = jnp.dot(left, pairs, preferred_element_type=jnp.float32).astype(jnp.bfloat16)
        rows = [
            jnp.concatenate(
                [middle[:VB, p * LANES : (p + 1) * LANES], middle[VB:, p * LANES : (p + 1) * LANES]],
                axis=1,
            )
            for p in range(2)
        ]
        term = lax.dot_general(
            jnp.concatenate(rows, axis=0),
            held[h, v, 1],
            (((1,), (1,)), ((), ())),
            preferred_element_type=jnp.float32,
        )
        total = term if total is None else total + term
    flat = [
        jnp.concatenate([total[p * VB : p * VB + 32], total[p * VB + 32 : (p + 1) * VB]], axis=1)
        for p in range(2)
    ]
    return jnp.concatenate(flat, axis=0)


def ladder_kernel(places, more, buffer, *refs):
    n = len(places)
    sources, earlier_ref = refs[:n], refs[n] if more else None
    out_ref, held, label_vmem, label_smem, sems, label_sem = refs[n + more : 6 + n + more]
    copies = [
        pltpu.make_async_copy(
            source, held.at[pl.ds(h, source.shape[0])] if len(source.shape) > 4 else held.at[h], sems.at[k]
        )
        for k, (source, h) in enumerate(zip(sources, places))
    ]
    for copy in copies:
        copy.start()
    read_labels(buffer, label_vmem, label_smem, label_sem)
    for copy in copies:
        copy.wait()

    if not more:

        def some(j, carry):
            for k in range(UNROLL):
                i = j * UNROLL + k
                out_ref[i] = slot_terms(i, label_smem, buffer, held)
            return carry

        lax.fori_loop(0, out_ref.shape[0] // UNROLL, some, 0)
        return

    done, out_sems = refs[6 + n + more :]
    slots = done.shape[0]
    outs = [
        pltpu.make_async_copy(done.at[pl.ds(k, OUT_SLOTS)], out_ref.at[pl.ds(k, OUT_SLOTS)], out_sems.at[k // OUT_SLOTS])
        for k in range(0, slots, OUT_SLOTS)
    ]
    for i in range(slots):
        done[i] = (slot_terms(i, label_smem, buffer, held) + earlier_ref[i]).astype(done.dtype)
        if i % OUT_SLOTS == OUT_SLOTS - 1:
            outs[i // OUT_SLOTS].start()
    for copy in outs:
        copy.wait()


def ladder_terms(buffer, factors, earlier=None):
    slots = buffer.shape[0] * CAP
    n, more = len(factors), int(earlier is not None)
    counts = [f.shape[0] if len(f.shape) > 4 else 1 for f in factors]
    places = [sum(counts[:k]) for k in range(n)]
    vmem, anywhere = pl.BlockSpec(memory_space=pltpu.VMEM), pl.BlockSpec(memory_space=pl.ANY)
    scratch = [
        pltpu.VMEM((sum(counts),) + factors[0].shape[-4:], factors[0].dtype),
        pltpu.VMEM((LABEL_ROWS, LANES), jnp.int32),
        pltpu.SMEM((LABEL_ROWS, LANES), jnp.int32),
        pltpu.SemaphoreType.DMA((n,)),
        pltpu.SemaphoreType.DMA,
    ]
    if more:
        scratch.append(pltpu.VMEM((slots, VB, LANES), jnp.bfloat16))
        scratch.append(pltpu.SemaphoreType.DMA((slots // OUT_SLOTS,)))
    return pl.pallas_call(
        lambda *refs: ladder_kernel(places, more, *refs),
        out_shape=jax.ShapeDtypeStruct((slots, VB, LANES), jnp.bfloat16 if more else jnp.float32),
        in_specs=[vmem] + [anywhere] * n + [vmem] * more,
        out_specs=anywhere if more else vmem,
        scratch_shapes=scratch,
        compiler_params=pltpu.CompilerParams(vmem_limit_bytes=LADDER_VMEM),
        cost_estimate=pl.CostEstimate(flops=10**7, bytes_accessed=sum(counts) << 19, transcendentals=0),
        name="ladder_terms",
    )(buffer, *factors, *([earlier] if more else []))


def finish_kernel(slot_ref, returned_ref, cycle_ref, out_ref, scratch):
    for g in range(out_ref.shape[0] // 4):
        spot = g % 2
        for j in range(4):
            block = returned_ref[slot_ref[4 * g + j]].astype(jnp.float32)
            for p in range(2):
                scratch[spot, pl.ds(2 * j + p, 32, stride=8), :] = block[p * 32 : (p + 1) * 32]
        for t in range(32):
            lanes = slice(t * LANES, (t + 1) * LANES)
            total = scratch[spot, 8 * t : 8 * t + 8, :] + cycle_ref[8 * g : 8 * g + 8, lanes]
            for j in range(4):
                out_ref[4 * g + j, :, lanes] = total[2 * j : 2 * j + 2].astype(jnp.bfloat16)


def finish(slot, returned, cycle):
    vmem = pl.BlockSpec(memory_space=pltpu.VMEM)
    return pl.pallas_call(
        finish_kernel,
        out_shape=jax.ShapeDtypeStruct((cycle.shape[0] // 2, 2, cycle.shape[1]), jnp.bfloat16),
        in_specs=[pl.BlockSpec(memory_space=pltpu.SMEM), vmem, vmem],
        out_specs=vmem,
        scratch_shapes=[pltpu.VMEM((2, 256, LANES), jnp.float32)],
        compiler_params=pltpu.CompilerParams(vmem_limit_bytes=SMALL_VMEM),
        name="finish_tiles",
    )(slot, returned, cycle)


def cycle_terms(lead, share, amplitudes, tile_blocks, live_rows, cycle_coupling):
    tiles, rows, cells = amplitudes.shape
    chosen = (tile_blocks[:, 0:1] == jnp.arange(cycle_coupling.shape[0])[None, :]).astype(jnp.bfloat16)
    mine = lax.dynamic_slice_in_dim(cycle_coupling, lead, share, 1)
    coupling = jnp.einsum("kn,npq->kpq", chosen, mine, preferred_element_type=jnp.float32)
    live = jnp.arange(rows)[None, :] < live_rows[:, None]
    same = jnp.eye(tiles, dtype=bool)
    mixing = jnp.where(
        same[:, None, :, None] & live[:, None, None, :], coupling[:, :, None, :], 0.0
    ).astype(jnp.bfloat16)
    return jnp.dot(
        mixing.reshape(tiles * share, tiles * rows),
        amplitudes.reshape(tiles * rows, cells),
        preferred_element_type=jnp.float32,
    )


def local(amplitudes, tile_blocks, live_rows, ladder_factors, cycle_coupling, block_owner):
    peers = lax.axis_size("tile")
    reps = lax.axis_size("rep")
    share = amplitudes.shape[1] // reps
    lead = lax.axis_index("rep") * share
    up = [(i, (i + 1) % reps) for i in range(reps)]
    down = [(i, (i - 1) % reps) for i in range(reps)]

    own, second = arrange_factors(ladder_factors)
    below = lax.ppermute(own, "rep", up)
    above_second = lax.ppermute(second, "rep", down)
    far_second = lax.ppermute(relay(above_second), "rep", down)
    above_first = lax.ppermute(own[0], "rep", down)
    far_first = lax.ppermute(below[0], "rep", up)

    packed, slot = pack(
        lead.astype(jnp.int32).reshape(1), tile_blocks.T, live_rows, block_owner, amplitudes, peers
    )
    buffer = lax.all_to_all(packed, "tile", split_axis=0, concat_axis=0, tiled=True)
    earlier = ladder_terms(buffer, (own, below, above_second, above_first))
    terms = ladder_terms(buffer, (far_second, far_first), earlier)
    tile_blocks, live_rows, terms = lax.optimization_barrier((tile_blocks, live_rows, terms))
    cycle = cycle_terms(lead, share, amplitudes, tile_blocks, live_rows, cycle_coupling)
    returned = lax.all_to_all(terms, "tile", split_axis=0, concat_axis=0, tiled=True)
    return finish(slot, returned, cycle)


def solution(mesh):
    placed = (
        P(("grp", "tile"), None, None),
        P(("grp", "tile"), None),
        P(("grp", "tile")),
        P("tile", None, "rep", None),
        P(),
        P(),
    )
    return jax.shard_map(
        local,
        mesh=mesh,
        in_specs=placed,
        out_specs=P(("grp", "tile"), "rep", None),
        check_vma=False,
    )
```

```python
import jax
import jax.numpy as jnp
from jax import lax
from jax.experimental import pallas as pl
from jax.experimental.pallas import tpu as pltpu
from jax.sharding import PartitionSpec as P

VB = 64
CAP = 2
GROUP = 4
LANES = 128
LABEL_ROWS = 16
FAR_UP = 9
CHUNK = 8
UNROLL = 32
PIECE = 16
OUT_SLOTS = 8
PACK_VMEM = 57 * 1024 * 1024
SMALL_VMEM = 16 * 1024 * 1024
LADDER_VMEM = 40 * 1024 * 1024


def low_lanes(shape):
    return lax.broadcasted_iota(jnp.int32, shape, 1) < VB


def join(first, second):
    low = low_lanes(first.shape)
    return (
        jnp.where(low, first, pltpu.roll(second, VB, 1)),
        jnp.where(low, pltpu.roll(first, VB, 1), second),
    )


def spread_rows(block, scratch):
    for t in range(block.shape[1] // LANES):
        scratch[t * 8 : (t + 1) * 8, :] = block[:, t * LANES : (t + 1) * LANES]


def factor_kernel(factor_ref, out_ref, scratch, woven):
    def one(v, carry):
        for side in range(2):
            spread_rows(factor_ref[v, side].astype(jnp.float32), scratch.at[side])
            for half in range(2):
                rows = [
                    scratch[side, pl.ds(half * GROUP + q, 32, stride=8), :] for q in range(GROUP)
                ]
                for pair in range(GROUP // 2):
                    even, odd = join(rows[2 * pair], rows[2 * pair + 1])
                    lanes = slice(pair * LANES, (pair + 1) * LANES)
                    if side == 0:
                        out_ref[2 * v + half, 0, 0:32, lanes] = even.astype(jnp.bfloat16)
                        out_ref[2 * v + half, 0, 32:64, lanes] = odd.astype(jnp.bfloat16)
                    else:
                        spot = half * 2 + pair
                        woven[spot, pl.ds(0, 32, stride=2), :] = even
                        woven[spot, pl.ds(1, 32, stride=2), :] = odd
                        out_ref[2 * v + half, 1, :, lanes] = woven[spot].astype(jnp.bfloat16)
        return carry

    lax.fori_loop(0, factor_ref.shape[0], one, 0, unroll=4)


def arrange_factors(factors):
    owned = factors.shape[0]
    return pl.pallas_call(
        factor_kernel,
        out_shape=jax.ShapeDtypeStruct((2 * owned, 2, VB, GROUP * VB), jnp.bfloat16),
        in_specs=[pl.BlockSpec(memory_space=pltpu.VMEM)],
        out_specs=pl.BlockSpec(memory_space=pltpu.VMEM),
        scratch_shapes=[
            pltpu.VMEM((2, 256, LANES), jnp.float32),
            pltpu.VMEM((4, VB, LANES), jnp.float32),
        ],
        compiler_params=pltpu.CompilerParams(vmem_limit_bytes=SMALL_VMEM),
        name="arrange_factors",
    )(factors)


def pack_kernel(
    lead_ref, blocks_hbm, live_hbm, owner_hbm, amp_hbm, out_ref, slot_ref,
    blocks_ref, live_ref, owner_ref, amp_ref, counts, labels, scratch, woven, sems,
):
    tables = [
        pltpu.make_async_copy(source, place, sems.at[k])
        for k, (source, place) in enumerate(
            ((blocks_hbm, blocks_ref), (live_hbm, live_ref), (owner_hbm, owner_ref))
        )
    ]
    tiles = amp_ref.shape[0]
    parts = [
        pltpu.make_async_copy(amp_hbm.at[pl.ds(k, CHUNK)], amp_ref.at[pl.ds(k, CHUNK)], sems.at[3 + k // CHUNK])
        for k in range(0, tiles, CHUNK)
    ]
    for copy in tables + parts:
        copy.start()
    peers = out_ref.shape[0]
    for s in range(peers):
        counts[s] = 0
        for r in range(CAP):
            labels[s, r] = 0
    out_ref[...] = jnp.zeros(out_ref.shape, out_ref.dtype)
    for copy in tables:
        copy.wait()
    owned = owner_ref.shape[0] // peers
    lead = lead_ref[0]
    for k in range(tiles):
        if k % CHUNK == 0:
            parts[k // CHUNK].wait()
        place = owner_ref[blocks_ref[1, k]]
        target = place // owned
        rank = counts[target]
        counts[target] = rank + 1
        labels[target, rank] = place - target * owned
        slot_ref[k] = target * CAP + rank
        spot = k % 2
        spread_rows(amp_ref[k].astype(jnp.float32), scratch.at[spot])
        live = live_ref[k]
        rows = [
            jnp.where(lead + p < live, scratch[spot, pl.ds(lead + p, 32, stride=8), :], 0.0)
            for p in range(2)
        ]
        even, odd = join(rows[0], rows[1])
        woven[spot, pl.ds(0, 32, stride=2), :] = even
        woven[spot, pl.ds(1, 32, stride=2), :] = odd
        out_ref[target, pl.ds(pl.multiple_of(rank * VB, VB), VB), :] = woven[spot].astype(jnp.bfloat16)
    row = lax.broadcasted_iota(jnp.int32, (LABEL_ROWS, LANES), 0)
    for s in range(peers):
        tag = jnp.where(row == 0, labels[s, 0], labels[s, 1])
        out_ref[s, CAP * VB :, :] = tag.astype(jnp.float32).astype(jnp.bfloat16)


def pack(lead, tile_blocks, live_rows, block_owner, amplitudes, peers):
    tiles = amplitudes.shape[0]
    smem = pl.BlockSpec(memory_space=pltpu.SMEM)
    vmem = pl.BlockSpec(memory_space=pltpu.VMEM)
    hbm = pl.BlockSpec(memory_space=pltpu.HBM)
    return pl.pallas_call(
        pack_kernel,
        out_shape=(
            jax.ShapeDtypeStruct((peers, CAP * VB + LABEL_ROWS, LANES), jnp.bfloat16),
            jax.ShapeDtypeStruct((tiles,), jnp.int32),
        ),
        in_specs=[smem, hbm, hbm, hbm, hbm],
        out_specs=(vmem, smem),
        scratch_shapes=[
            pltpu.SMEM(tile_blocks.shape, jnp.int32),
            pltpu.SMEM(live_rows.shape, jnp.int32),
            pltpu.SMEM(block_owner.shape, jnp.int32),
            pltpu.VMEM(amplitudes.shape, amplitudes.dtype),
            pltpu.SMEM((peers,), jnp.int32),
            pltpu.SMEM((peers, CAP), jnp.int32),
            pltpu.VMEM((2, 256, LANES), jnp.float32),
            pltpu.VMEM((2, VB, LANES), jnp.float32),
            pltpu.SemaphoreType.DMA((3 + tiles // CHUNK,)),
        ],
        compiler_params=pltpu.CompilerParams(vmem_limit_bytes=PACK_VMEM),
        name="pack_tiles",
    )(lead, tile_blocks, live_rows, block_owner, amplitudes)


def read_labels(buffer_ref, label_vmem, label_smem, sem):
    lane = lax.broadcasted_iota(jnp.int32, (LABEL_ROWS, LANES), 1)
    table = jnp.zeros((LABEL_ROWS, LANES), jnp.float32)
    for s in range(buffer_ref.shape[0]):
        table = jnp.where(lane == s, buffer_ref[s, CAP * VB :, :].astype(jnp.float32), table)
    label_vmem[...] = table.astype(jnp.int32)
    copy = pltpu.make_async_copy(label_vmem, label_smem, sem)
    copy.start()
    copy.wait()


def slot_terms(i, label_smem, buffer, held):
    peer, rank = i // CAP, i % CAP
    v = label_smem[rank, peer]
    tile = buffer[peer, pl.ds(pl.multiple_of(rank * VB, VB), VB), :].astype(jnp.float32)
    turned = pltpu.roll(tile, VB, 1)
    low = low_lanes(tile.shape)
    upper = [jnp.where(low, rows, 0.0).astype(jnp.bfloat16) for rows in (tile, turned)]
    lower = [jnp.where(low, 0.0, rows).astype(jnp.bfloat16) for rows in (turned, tile)]
    pairs = jnp.concatenate([jnp.concatenate(upper, axis=1), jnp.concatenate(lower, axis=1)], axis=0)
    total = None
    for h, half in [(h, half) for h in range(held.shape[0]) for half in range(2)]:
        left = held[h, 2 * v + half, 0]
        left = jnp.concatenate([left[:, :LANES], left[:, LANES:]], axis=0)
        middle = jnp.dot(left, pairs, preferred_element_type=jnp.float32).astype(jnp.bfloat16)
        rows = [
            jnp.concatenate(
                [middle[:VB, p * LANES : (p + 1) * LANES], middle[VB:, p * LANES : (p + 1) * LANES]],
                axis=1,
            )
            for p in range(2)
        ]
        term = lax.dot_general(
            jnp.concatenate(rows, axis=0),
            held[h, 2 * v + half, 1],
            (((1,), (1,)), ((), ())),
            preferred_element_type=jnp.float32,
        )
        total = term if total is None else total + term
    flat = [
        jnp.concatenate([total[p * VB : p * VB + 32], total[p * VB + 32 : (p + 1) * VB]], axis=1)
        for p in range(2)
    ]
    return jnp.concatenate(flat, axis=0)


def ladder_kernel(places, more, buffer, *refs):
    n = len(places)
    sources, earlier_ref = refs[:n], refs[n] if more else None
    out_ref, held, label_vmem, label_smem, sems, label_sem = refs[n + more : 6 + n + more]
    copies = []
    for source, (h, first) in zip(sources, places):
        for begin in range(0, source.shape[0], PIECE):
            count = min(PIECE, source.shape[0] - begin)
            copies.append(
                pltpu.make_async_copy(
                    source.at[pl.ds(begin, count)], held.at[h, pl.ds(first + begin, count)], sems.at[len(copies)]
                )
            )
    for copy in copies:
        copy.start()
    read_labels(buffer, label_vmem, label_smem, label_sem)
    for copy in copies:
        copy.wait()

    if not more:

        def some(j, carry):
            for k in range(UNROLL):
                i = j * UNROLL + k
                out_ref[i] = slot_terms(i, label_smem, buffer, held)
            return carry

        lax.fori_loop(0, out_ref.shape[0] // UNROLL, some, 0)
        return

    done, out_sems = refs[6 + n + more :]
    slots = done.shape[0]
    outs = [
        pltpu.make_async_copy(done.at[pl.ds(k, OUT_SLOTS)], out_ref.at[pl.ds(k, OUT_SLOTS)], out_sems.at[k // OUT_SLOTS])
        for k in range(0, slots, OUT_SLOTS)
    ]
    for i in range(slots):
        done[i] = (slot_terms(i, label_smem, buffer, held) + earlier_ref[i]).astype(done.dtype)
        if i % OUT_SLOTS == OUT_SLOTS - 1:
            outs[i // OUT_SLOTS].start()
    for copy in outs:
        copy.wait()


def ladder_terms(buffer, factors, places, earlier=None):
    slots = buffer.shape[0] * CAP
    n, more = len(factors), int(earlier is not None)
    shards = 1 + max(h for h, first in places)
    pieces = max(first + f.shape[0] for f, (h, first) in zip(factors, places))
    vmem, anywhere = pl.BlockSpec(memory_space=pltpu.VMEM), pl.BlockSpec(memory_space=pl.ANY)
    scratch = [
        pltpu.VMEM((shards, pieces) + factors[0].shape[1:], factors[0].dtype),
        pltpu.VMEM((LABEL_ROWS, LANES), jnp.int32),
        pltpu.SMEM((LABEL_ROWS, LANES), jnp.int32),
        pltpu.SemaphoreType.DMA((sum(-(-f.shape[0] // PIECE) for f in factors),)),
        pltpu.SemaphoreType.DMA,
    ]
    if more:
        scratch.append(pltpu.VMEM((slots, VB, LANES), jnp.bfloat16))
        scratch.append(pltpu.SemaphoreType.DMA((slots // OUT_SLOTS,)))
    return pl.pallas_call(
        lambda *refs: ladder_kernel(places, more, *refs),
        out_shape=jax.ShapeDtypeStruct((slots, VB, LANES), jnp.bfloat16 if more else jnp.float32),
        in_specs=[vmem] + [anywhere] * n + [vmem] * more,
        out_specs=anywhere if more else vmem,
        scratch_shapes=scratch,
        compiler_params=pltpu.CompilerParams(vmem_limit_bytes=LADDER_VMEM),
        cost_estimate=pl.CostEstimate(flops=10**7, bytes_accessed=shards << 20, transcendentals=0),
        name="ladder_terms",
    )(buffer, *factors, *([earlier] if more else []))


def finish_kernel(slot_ref, returned_ref, cycle_ref, out_ref, scratch):
    for g in range(out_ref.shape[0] // 4):
        spot = g % 2
        for j in range(4):
            block = returned_ref[slot_ref[4 * g + j]].astype(jnp.float32)
            for p in range(2):
                scratch[spot, pl.ds(2 * j + p, 32, stride=8), :] = block[p * 32 : (p + 1) * 32]
        for t in range(32):
            lanes = slice(t * LANES, (t + 1) * LANES)
            total = scratch[spot, 8 * t : 8 * t + 8, :] + cycle_ref[8 * g : 8 * g + 8, lanes]
            for j in range(4):
                out_ref[4 * g + j, :, lanes] = total[2 * j : 2 * j + 2].astype(jnp.bfloat16)


def finish(slot, returned, cycle):
    vmem = pl.BlockSpec(memory_space=pltpu.VMEM)
    return pl.pallas_call(
        finish_kernel,
        out_shape=jax.ShapeDtypeStruct((cycle.shape[0] // 2, 2, cycle.shape[1]), jnp.bfloat16),
        in_specs=[pl.BlockSpec(memory_space=pltpu.SMEM), vmem, vmem],
        out_specs=vmem,
        scratch_shapes=[pltpu.VMEM((2, 256, LANES), jnp.float32)],
        compiler_params=pltpu.CompilerParams(vmem_limit_bytes=SMALL_VMEM),
        name="finish_tiles",
    )(slot, returned, cycle)


def cycle_kernel(
    lead_ref, blocks_hbm, live_hbm, coupling_ref, amp_ref, after_ref, out_ref, held, mixing, blocks_ref, live_ref, sems
):
    tables = [
        pltpu.make_async_copy(blocks_hbm, blocks_ref, sems.at[0]),
        pltpu.make_async_copy(live_hbm, live_ref, sems.at[1]),
    ]
    for copy in tables:
        copy.start()
    tiles, rows, cells = amp_ref.shape
    lead = lead_ref[0]
    held[...] = jnp.zeros(held.shape, held.dtype)
    lane = lax.broadcasted_iota(jnp.int32, (rows, rows), 1)
    for copy in tables:
        copy.wait()
    for k in range(tiles):
        block = coupling_ref[blocks_ref[0, k]].astype(jnp.float32)
        held[k, :, 0:rows] = jnp.where(lane < live_ref[k], block, 0.0)
        for p in range(2):
            row = held[k, pl.ds(lead + p, 1), :]
            mixing[2 * k + p : 2 * k + p + 1, :] = pltpu.roll(row, rows * k, 1) if k else row
    mix = mixing[...].astype(jnp.bfloat16)
    for begin in range(0, cells, 512):
        lanes = slice(begin, begin + 512)
        out_ref[:, lanes] = jnp.dot(
            mix, amp_ref[:, :, lanes].reshape(tiles * rows, 512), preferred_element_type=jnp.float32
        )


def cycle_terms(lead, tile_blocks, live_rows, cycle_coupling, amplitudes, after):
    tiles, rows, cells = amplitudes.shape
    smem, vmem = pl.BlockSpec(memory_space=pltpu.SMEM), pl.BlockSpec(memory_space=pltpu.VMEM)
    hbm = pl.BlockSpec(memory_space=pltpu.HBM)
    return pl.pallas_call(
        cycle_kernel,
        out_shape=jax.ShapeDtypeStruct((2 * tiles, cells), jnp.float32),
        in_specs=[smem, hbm, hbm, vmem, vmem, pl.BlockSpec(memory_space=pl.ANY)],
        out_specs=vmem,
        scratch_shapes=[
            pltpu.VMEM((tiles, rows, LANES), jnp.float32),
            pltpu.VMEM((2 * tiles, LANES), jnp.float32),
            pltpu.SMEM(tile_blocks.shape, jnp.int32),
            pltpu.SMEM(live_rows.shape, jnp.int32),
            pltpu.SemaphoreType.DMA((2,)),
        ],
        compiler_params=pltpu.CompilerParams(vmem_limit_bytes=SMALL_VMEM),
        name="cycle_terms",
    )(lead, tile_blocks, live_rows, cycle_coupling, amplitudes, after)


def local(amplitudes, tile_blocks, live_rows, ladder_factors, cycle_coupling, block_owner):
    peers = lax.axis_size("tile")
    reps = lax.axis_size("rep")
    share = amplitudes.shape[1] // reps
    lead = (lax.axis_index("rep") * share).astype(jnp.int32).reshape(1)
    blocks = tile_blocks.T
    up = [(i, (i + 1) % reps) for i in range(reps)]
    down = [(i, (i - 1) % reps) for i in range(reps)]

    own = arrange_factors(ladder_factors)
    below = lax.ppermute(own, "rep", up)
    above = lax.ppermute(own, "rep", down)
    far_first = lax.ppermute(below[:FAR_UP], "rep", up)
    far_second = lax.ppermute(above[FAR_UP:], "rep", down)

    packed, slot = pack(lead, blocks, live_rows, block_owner, amplitudes, peers)
    buffer = lax.all_to_all(packed, "tile", split_axis=0, concat_axis=0, tiled=True)
    earlier = ladder_terms(buffer, (own, below, above), ((0, 0), (1, 0), (2, 0)))
    terms = ladder_terms(buffer, (far_first, far_second), ((0, 0), (0, FAR_UP)), earlier)
    cycle = cycle_terms(lead, blocks, live_rows, cycle_coupling, amplitudes, terms)
    returned = lax.all_to_all(terms, "tile", split_axis=0, concat_axis=0, tiled=True)
    return finish(slot, returned, cycle)


def solution(mesh):
    placed = (
        P(("grp", "tile"), None, None),
        P(("grp", "tile"), None),
        P(("grp", "tile")),
        P("tile", None, "rep", None),
        P(),
        P(),
    )
    return jax.shard_map(
        local,
        mesh=mesh,
        in_specs=placed,
        out_specs=P(("grp", "tile"), "rep", None),
        check_vma=False,
    )
```

```python
import jax
import jax.numpy as jnp
from jax import lax
from jax.experimental import pallas as pl
from jax.experimental.pallas import tpu as pltpu
from jax.sharding import PartitionSpec as P

VB = 64
CAP = 2
GROUP = 4
LANES = 128
LABEL_ROWS = 16
FAR_UP = 9
CHUNK = 8
UNROLL = 32
PIECE = 16
OUT_SLOTS = 8
PACK_VMEM = 57 * 1024 * 1024
SMALL_VMEM = 16 * 1024 * 1024
LADDER_VMEM = 40 * 1024 * 1024


def low_lanes(shape):
    return lax.broadcasted_iota(jnp.int32, shape, 1) < VB


def join(first, second):
    low = low_lanes(first.shape)
    return (
        jnp.where(low, first, pltpu.roll(second, VB, 1)),
        jnp.where(low, pltpu.roll(first, VB, 1), second),
    )


def spread_rows(block, scratch):
    for t in range(block.shape[1] // LANES):
        scratch[t * 8 : (t + 1) * 8, :] = block[:, t * LANES : (t + 1) * LANES]


def factor_kernel(factor_ref, out_ref, scratch, woven):
    def one(v, carry):
        for side in range(2):
            spread_rows(factor_ref[v, side].astype(jnp.float32), scratch.at[side])
            for half in range(2):
                rows = [
                    scratch[side, pl.ds(half * GROUP + q, 32, stride=8), :] for q in range(GROUP)
                ]
                for pair in range(GROUP // 2):
                    even, odd = join(rows[2 * pair], rows[2 * pair + 1])
                    lanes = slice(pair * LANES, (pair + 1) * LANES)
                    if side == 0:
                        out_ref[2 * v + half, 0, 0:32, lanes] = even.astype(jnp.bfloat16)
                        out_ref[2 * v + half, 0, 32:64, lanes] = odd.astype(jnp.bfloat16)
                    else:
                        spot = half * 2 + pair
                        woven[spot, pl.ds(0, 32, stride=2), :] = even
                        woven[spot, pl.ds(1, 32, stride=2), :] = odd
                        out_ref[2 * v + half, 1, :, lanes] = woven[spot].astype(jnp.bfloat16)
        return carry

    lax.fori_loop(0, factor_ref.shape[0], one, 0, unroll=8)


def arrange_factors(factors):
    owned = factors.shape[0]
    return pl.pallas_call(
        factor_kernel,
        out_shape=jax.ShapeDtypeStruct((2 * owned, 2, VB, GROUP * VB), jnp.bfloat16),
        in_specs=[pl.BlockSpec(memory_space=pltpu.VMEM)],
        out_specs=pl.BlockSpec(memory_space=pltpu.VMEM),
        scratch_shapes=[
            pltpu.VMEM((2, 256, LANES), jnp.float32),
            pltpu.VMEM((4, VB, LANES), jnp.float32),
        ],
        compiler_params=pltpu.CompilerParams(vmem_limit_bytes=SMALL_VMEM),
        name="arrange_factors",
    )(factors)


def pack_kernel(
    lead_ref, blocks_hbm, live_hbm, owner_hbm, amp_hbm, out_ref, slot_ref,
    blocks_ref, live_ref, owner_ref, amp_ref, counts, labels, scratch, woven, sems,
):
    tables = [
        pltpu.make_async_copy(source, place, sems.at[k])
        for k, (source, place) in enumerate(
            ((blocks_hbm, blocks_ref), (live_hbm, live_ref), (owner_hbm, owner_ref))
        )
    ]
    tiles = amp_ref.shape[0]
    parts = [
        pltpu.make_async_copy(amp_hbm.at[pl.ds(k, CHUNK)], amp_ref.at[pl.ds(k, CHUNK)], sems.at[3 + k // CHUNK])
        for k in range(0, tiles, CHUNK)
    ]
    for copy in tables + parts:
        copy.start()
    peers = out_ref.shape[0]
    for s in range(peers):
        counts[s] = 0
        for r in range(CAP):
            labels[s, r] = 0
    out_ref[...] = jnp.zeros(out_ref.shape, out_ref.dtype)
    for copy in tables:
        copy.wait()
    owned = owner_ref.shape[0] // peers
    lead = lead_ref[0]
    for k in range(tiles):
        if k % CHUNK == 0:
            parts[k // CHUNK].wait()
        place = owner_ref[blocks_ref[1, k]]
        target = place // owned
        rank = counts[target]
        counts[target] = rank + 1
        labels[target, rank] = place - target * owned
        slot_ref[k] = target * CAP + rank
        spot = k % 2
        spread_rows(amp_ref[k].astype(jnp.float32), scratch.at[spot])
        live = live_ref[k]
        rows = [
            jnp.where(lead + p < live, scratch[spot, pl.ds(lead + p, 32, stride=8), :], 0.0)
            for p in range(2)
        ]
        even, odd = join(rows[0], rows[1])
        woven[spot, pl.ds(0, 32, stride=2), :] = even
        woven[spot, pl.ds(1, 32, stride=2), :] = odd
        out_ref[target, pl.ds(pl.multiple_of(rank * VB, VB), VB), :] = woven[spot].astype(jnp.bfloat16)
    row = lax.broadcasted_iota(jnp.int32, (LABEL_ROWS, LANES), 0)
    for s in range(peers):
        tag = jnp.where(row == 0, labels[s, 0], labels[s, 1])
        out_ref[s, CAP * VB :, :] = tag.astype(jnp.float32).astype(jnp.bfloat16)


def pack(lead, tile_blocks, live_rows, block_owner, amplitudes, peers):
    tiles = amplitudes.shape[0]
    smem = pl.BlockSpec(memory_space=pltpu.SMEM)
    vmem = pl.BlockSpec(memory_space=pltpu.VMEM)
    hbm = pl.BlockSpec(memory_space=pltpu.HBM)
    return pl.pallas_call(
        pack_kernel,
        out_shape=(
            jax.ShapeDtypeStruct((peers, CAP * VB + LABEL_ROWS, LANES), jnp.bfloat16),
            jax.ShapeDtypeStruct((tiles,), jnp.int32),
        ),
        in_specs=[smem, hbm, hbm, hbm, hbm],
        out_specs=(vmem, smem),
        scratch_shapes=[
            pltpu.SMEM(tile_blocks.shape, jnp.int32),
            pltpu.SMEM(live_rows.shape, jnp.int32),
            pltpu.SMEM(block_owner.shape, jnp.int32),
            pltpu.VMEM(amplitudes.shape, amplitudes.dtype),
            pltpu.SMEM((peers,), jnp.int32),
            pltpu.SMEM((peers, CAP), jnp.int32),
            pltpu.VMEM((2, 256, LANES), jnp.float32),
            pltpu.VMEM((2, VB, LANES), jnp.float32),
            pltpu.SemaphoreType.DMA((3 + tiles // CHUNK,)),
        ],
        compiler_params=pltpu.CompilerParams(vmem_limit_bytes=PACK_VMEM),
        name="pack_tiles",
    )(lead, tile_blocks, live_rows, block_owner, amplitudes)


def read_labels(buffer_ref, label_vmem, label_smem, sem):
    lane = lax.broadcasted_iota(jnp.int32, (LABEL_ROWS, LANES), 1)
    table = jnp.zeros((LABEL_ROWS, LANES), jnp.float32)
    for s in range(buffer_ref.shape[0]):
        table = jnp.where(lane == s, buffer_ref[s, CAP * VB :, :].astype(jnp.float32), table)
    label_vmem[...] = table.astype(jnp.int32)
    copy = pltpu.make_async_copy(label_vmem, label_smem, sem)
    copy.start()
    copy.wait()


def slot_terms(i, label_smem, buffer, held):
    peer, rank = i // CAP, i % CAP
    v = label_smem[rank, peer]
    tile = buffer[peer, pl.ds(pl.multiple_of(rank * VB, VB), VB), :].astype(jnp.float32)
    turned = pltpu.roll(tile, VB, 1)
    low = low_lanes(tile.shape)
    upper = [jnp.where(low, rows, 0.0).astype(jnp.bfloat16) for rows in (tile, turned)]
    lower = [jnp.where(low, 0.0, rows).astype(jnp.bfloat16) for rows in (turned, tile)]
    pairs = jnp.concatenate([jnp.concatenate(upper, axis=1), jnp.concatenate(lower, axis=1)], axis=0)
    total = None
    for h, half in [(h, half) for h in range(held.shape[0]) for half in range(2)]:
        left = held[h, 2 * v + half, 0]
        left = jnp.concatenate([left[:, :LANES], left[:, LANES:]], axis=0)
        middle = jnp.dot(left, pairs, preferred_element_type=jnp.float32).astype(jnp.bfloat16)
        rows = [
            jnp.concatenate(
                [middle[:VB, p * LANES : (p + 1) * LANES], middle[VB:, p * LANES : (p + 1) * LANES]],
                axis=1,
            )
            for p in range(2)
        ]
        term = lax.dot_general(
            jnp.concatenate(rows, axis=0),
            held[h, 2 * v + half, 1],
            (((1,), (1,)), ((), ())),
            preferred_element_type=jnp.float32,
        )
        total = term if total is None else total + term
    flat = [
        jnp.concatenate([total[p * VB : p * VB + 32], total[p * VB + 32 : (p + 1) * VB]], axis=1)
        for p in range(2)
    ]
    return jnp.concatenate(flat, axis=0)


def ladder_kernel(places, more, buffer, *refs):
    n = len(places)
    sources, earlier_ref = refs[:n], refs[n] if more else None
    out_ref, held, label_vmem, label_smem, sems, label_sem = refs[n + more : 6 + n + more]
    copies = []
    for source, (h, first) in zip(sources, places):
        for begin in range(0, source.shape[0], PIECE):
            count = min(PIECE, source.shape[0] - begin)
            copies.append(
                pltpu.make_async_copy(
                    source.at[pl.ds(begin, count)], held.at[h, pl.ds(first + begin, count)], sems.at[len(copies)]
                )
            )
    for copy in copies:
        copy.start()
    read_labels(buffer, label_vmem, label_smem, label_sem)
    for copy in copies:
        copy.wait()

    if not more:

        def some(j, carry):
            for k in range(UNROLL):
                i = j * UNROLL + k
                out_ref[i] = slot_terms(i, label_smem, buffer, held)
            return carry

        lax.fori_loop(0, out_ref.shape[0] // UNROLL, some, 0)
        return

    done, out_sems = refs[6 + n + more :]
    slots = done.shape[0]
    outs = [
        pltpu.make_async_copy(done.at[pl.ds(k, OUT_SLOTS)], out_ref.at[pl.ds(k, OUT_SLOTS)], out_sems.at[k // OUT_SLOTS])
        for k in range(0, slots, OUT_SLOTS)
    ]
    for i in range(slots):
        done[i] = (slot_terms(i, label_smem, buffer, held) + earlier_ref[i]).astype(done.dtype)
        if i % OUT_SLOTS == OUT_SLOTS - 1:
            outs[i // OUT_SLOTS].start()
    for copy in outs:
        copy.wait()


def ladder_terms(buffer, factors, places, earlier=None):
    slots = buffer.shape[0] * CAP
    n, more = len(factors), int(earlier is not None)
    shards = 1 + max(h for h, first in places)
    pieces = max(first + f.shape[0] for f, (h, first) in zip(factors, places))
    vmem, anywhere = pl.BlockSpec(memory_space=pltpu.VMEM), pl.BlockSpec(memory_space=pl.ANY)
    scratch = [
        pltpu.VMEM((shards, pieces) + factors[0].shape[1:], factors[0].dtype),
        pltpu.VMEM((LABEL_ROWS, LANES), jnp.int32),
        pltpu.SMEM((LABEL_ROWS, LANES), jnp.int32),
        pltpu.SemaphoreType.DMA((sum(-(-f.shape[0] // PIECE) for f in factors),)),
        pltpu.SemaphoreType.DMA,
    ]
    if more:
        scratch.append(pltpu.VMEM((slots, VB, LANES), jnp.bfloat16))
        scratch.append(pltpu.SemaphoreType.DMA((slots // OUT_SLOTS,)))
    return pl.pallas_call(
        lambda *refs: ladder_kernel(places, more, *refs),
        out_shape=jax.ShapeDtypeStruct((slots, VB, LANES), jnp.bfloat16 if more else jnp.float32),
        in_specs=[vmem] + [anywhere] * n + [vmem] * more,
        out_specs=anywhere if more else vmem,
        scratch_shapes=scratch,
        compiler_params=pltpu.CompilerParams(vmem_limit_bytes=LADDER_VMEM),
        cost_estimate=pl.CostEstimate(flops=10**7, bytes_accessed=shards << 20, transcendentals=0),
        name="ladder_terms",
    )(buffer, *factors, *([earlier] if more else []))


def finish_kernel(slot_ref, returned_ref, cycle_ref, out_ref, scratch):
    for g in range(out_ref.shape[0] // 4):
        spot = g % 2
        for j in range(4):
            block = returned_ref[slot_ref[4 * g + j]].astype(jnp.float32)
            for p in range(2):
                scratch[spot, pl.ds(2 * j + p, 32, stride=8), :] = block[p * 32 : (p + 1) * 32]
        for t in range(32):
            lanes = slice(t * LANES, (t + 1) * LANES)
            total = scratch[spot, 8 * t : 8 * t + 8, :] + cycle_ref[8 * g : 8 * g + 8, lanes]
            for j in range(4):
                out_ref[4 * g + j, :, lanes] = total[2 * j : 2 * j + 2].astype(jnp.bfloat16)


def finish(slot, returned, cycle):
    vmem = pl.BlockSpec(memory_space=pltpu.VMEM)
    return pl.pallas_call(
        finish_kernel,
        out_shape=jax.ShapeDtypeStruct((cycle.shape[0] // 2, 2, cycle.shape[1]), jnp.bfloat16),
        in_specs=[pl.BlockSpec(memory_space=pltpu.SMEM), vmem, vmem],
        out_specs=vmem,
        scratch_shapes=[pltpu.VMEM((2, 256, LANES), jnp.float32)],
        compiler_params=pltpu.CompilerParams(vmem_limit_bytes=SMALL_VMEM),
        name="finish_tiles",
    )(slot, returned, cycle)


def cycle_kernel(
    lead_ref, blocks_hbm, live_hbm, coupling_ref, amp_ref, after_ref, out_ref, held, mixing, blocks_ref, live_ref, sems
):
    tables = [
        pltpu.make_async_copy(blocks_hbm, blocks_ref, sems.at[0]),
        pltpu.make_async_copy(live_hbm, live_ref, sems.at[1]),
    ]
    for copy in tables:
        copy.start()
    tiles, rows, cells = amp_ref.shape
    lead = lead_ref[0]
    held[...] = jnp.zeros(held.shape, held.dtype)
    lane = lax.broadcasted_iota(jnp.int32, (rows, rows), 1)
    for copy in tables:
        copy.wait()
    for k in range(tiles):
        block = coupling_ref[blocks_ref[0, k]].astype(jnp.float32)
        held[k, :, 0:rows] = jnp.where(lane < live_ref[k], block, 0.0)
        for p in range(2):
            row = held[k, pl.ds(lead + p, 1), :]
            mixing[2 * k + p : 2 * k + p + 1, :] = pltpu.roll(row, rows * k, 1) if k else row
    mix = mixing[...].astype(jnp.bfloat16)
    for begin in range(0, cells, 512):
        lanes = slice(begin, begin + 512)
        out_ref[:, lanes] = jnp.dot(
            mix, amp_ref[:, :, lanes].reshape(tiles * rows, 512), preferred_element_type=jnp.float32
        )


def cycle_terms(lead, tile_blocks, live_rows, cycle_coupling, amplitudes, after):
    tiles, rows, cells = amplitudes.shape
    smem, vmem = pl.BlockSpec(memory_space=pltpu.SMEM), pl.BlockSpec(memory_space=pltpu.VMEM)
    hbm = pl.BlockSpec(memory_space=pltpu.HBM)
    return pl.pallas_call(
        cycle_kernel,
        out_shape=jax.ShapeDtypeStruct((2 * tiles, cells), jnp.float32),
        in_specs=[smem, hbm, hbm, vmem, vmem, pl.BlockSpec(memory_space=pl.ANY)],
        out_specs=vmem,
        scratch_shapes=[
            pltpu.VMEM((tiles, rows, LANES), jnp.float32),
            pltpu.VMEM((2 * tiles, LANES), jnp.float32),
            pltpu.SMEM(tile_blocks.shape, jnp.int32),
            pltpu.SMEM(live_rows.shape, jnp.int32),
            pltpu.SemaphoreType.DMA((2,)),
        ],
        compiler_params=pltpu.CompilerParams(vmem_limit_bytes=SMALL_VMEM),
        name="cycle_terms",
    )(lead, tile_blocks, live_rows, cycle_coupling, amplitudes, after)


def local(amplitudes, tile_blocks, live_rows, ladder_factors, cycle_coupling, block_owner):
    peers = lax.axis_size("tile")
    reps = lax.axis_size("rep")
    share = amplitudes.shape[1] // reps
    lead = (lax.axis_index("rep") * share).astype(jnp.int32).reshape(1)
    blocks = tile_blocks.T
    up = [(i, (i + 1) % reps) for i in range(reps)]
    down = [(i, (i - 1) % reps) for i in range(reps)]

    own = arrange_factors(ladder_factors)
    below = lax.ppermute(own, "rep", up)
    above = lax.ppermute(own, "rep", down)
    far_first = lax.ppermute(below[:FAR_UP], "rep", up)
    far_second = lax.ppermute(above[FAR_UP:], "rep", down)

    packed, slot = pack(lead, blocks, live_rows, block_owner, amplitudes, peers)
    buffer = lax.all_to_all(packed, "tile", split_axis=0, concat_axis=0, tiled=True)
    earlier = ladder_terms(buffer, (own, below, above), ((0, 0), (1, 0), (2, 0)))
    terms = ladder_terms(buffer, (far_first, far_second), ((0, 0), (0, FAR_UP)), earlier)
    cycle = cycle_terms(lead, blocks, live_rows, cycle_coupling, amplitudes, terms)
    returned = lax.all_to_all(terms, "tile", split_axis=0, concat_axis=0, tiled=True)
    return finish(slot, returned, cycle)


def solution(mesh):
    placed = (
        P(("grp", "tile"), None, None),
        P(("grp", "tile"), None),
        P(("grp", "tile")),
        P("tile", None, "rep", None),
        P(),
        P(),
    )
    return jax.shard_map(
        local,
        mesh=mesh,
        in_specs=placed,
        out_specs=P(("grp", "tile"), "rep", None),
        check_vma=False,
    )
```
